256 devices in a mesh: blk: 32 (over x_hi, z, core), grp: 8 (over y, x_lo).
Axes of the slice: x: 4 (x_hi: 2, x_lo: 2; x = x_hi * 2 + x_lo), y: 4, z: 8, core: 2. Of those that a mesh axis runs over, the one named last changes fastest.
Arguments:
- embedding: bfloat16 [262144, 512], P(('blk', 'grp')), may hold values from -2 to 2
- direction: float32 [262144, 32], P(('blk', 'grp'))
- residual: float32 [262144, 32], P(('blk', 'grp'))
- solution: float32 [262144, 32], P(('blk', 'grp')), may hold values from -6 to 6
- prior: float32 [262144, 32], P(('blk', 'grp')), may hold values from -6 to 6
- plan: int32 [255], replicated, may hold values from 1 to 255, as said below
- round_index: int32 [1], replicated, may hold values from 0 to 252
Outputs:
- new_solution: float32 [262144, 32], P(('blk', 'grp'))
- new_residual: float32 [262144, 32], P(('blk', 'grp'))
- new_direction: float32 [262144, 32], P(('blk', 'grp'))
The draws below stay inside these ranges and needn't reach their ends.
Inputs may be any that keep to these rules, and one draw needn't show every extreme that they name: `plan`: every value 1 to 255 appears exactly once.
All inputs are finite; a program needn't handle non-finite values.
Results may differ from the reference program's by a relative error of at most 0.0049.
Values may be sent and summed in bfloat16 or wider, within the bound.
A program may use at most 64 MiB of HBM per device.

```python
import math
import jax
import jax.numpy as jnp
from jax import lax

D = 512
PROBES = 32
ROWS = 1024
ROUNDS = 3
BLOCKS = 256
NPTS = 262144


def scaled_field(key, rising):
    position = jnp.arange(NPTS, dtype=jnp.float32) / (NPTS - 1.0)
    jitter = jnp.exp(jax.random.uniform(jax.random.fold_in(key, 11), (NPTS, 1), jnp.float32, -0.5, 0.5))
    profile = (rising ** position)[:, None] * jitter
    values = jax.random.normal(jax.random.fold_in(key, 13), (NPTS, PROBES), jnp.float32)
    return values * profile


def feature_field(key, strong_count, strong_total, base):
    order = jax.random.permutation(jax.random.fold_in(key, 23), D)
    strong = order < strong_count
    strong_scale = math.sqrt(strong_total / strong_count)
    weak_scale = math.sqrt(0.1 / (D - strong_count))
    scales = jnp.where(strong, strong_scale, weak_scale).astype(jnp.float32)
    return jnp.clip(base * scales[None, :], -2.0, 2.0)


def draw_direction(key, part):
    key = jax.random.fold_in(key, 1)
    return scaled_field(key, 3.0)


def draw_residual(key, part):
    key = jax.random.fold_in(key, 2)
    return scaled_field(key, 3.0)


def draw_plan(key, part):
    key = jax.random.fold_in(key, 3)
    return (jax.random.permutation(key, BLOCKS - 1) + 1).astype(jnp.int32)


def draw_embedding(key, part):
    key = jax.random.fold_in(key, 4)
    base = jax.random.normal(jax.random.fold_in(key, 22), (NPTS, D), jnp.float32)
    return feature_field(key, max(D // 32, 1), 0.64, base).astype(jnp.bfloat16)


def level_of(own_key, extent, cuts, low, high):
    def one(dim, blocks):
        draws = jax.random.uniform(jax.random.fold_in(jax.random.fold_in(own_key, 6), dim), (blocks,), jnp.float32, low / len(cuts), high / len(cuts))
        return jnp.repeat(jnp.exp(draws), extent[dim] // blocks).reshape((-1,) + (1,) * (len(extent) - dim - 1))

    level = one(*cuts[0])
    for cut in cuts[1:]:
        level = level * one(*cut)
    return level


def normal_values(stream_key, extent, deviation, limit, cuts=(), kind=jnp.bfloat16):
    factor_of = level_of(stream_key, extent, cuts, -0.22, 0.18) if cuts else 1.0
    values = jax.random.normal(stream_key, extent, jnp.float32) * deviation * factor_of
    return jnp.minimum(jnp.maximum(values, -limit), limit).astype(kind)


def setup_inputs(seed: int = 0) -> dict:
    splits = jax.random.split(jax.random.key(seed), 8)
    return {
        "embedding": draw_embedding(jax.random.fold_in(splits[7], 71), 0),
        "direction": draw_direction(jax.random.fold_in(splits[7], 71), 0),
        "residual": draw_residual(jax.random.fold_in(splits[7], 71), 0),
        "solution": normal_values(splits[3], (NPTS, PROBES), 1.0, 6.0, ((0, 256),), jnp.float32),
        "prior": normal_values(splits[4], (NPTS, PROBES), 1.0, 6.0, ((0, 256),), jnp.float32),
        "plan": draw_plan(jax.random.fold_in(splits[7], 71), 0),
        "round_index": jax.random.randint(splits[6], (1,), 0, BLOCKS - 3).astype(jnp.int32),
    }


AMPLITUDE = 2.0
GAMMA = 2.0
NOISE = 1.0


def kernel_block(left, left_sq, right, right_sq):
    cross = jnp.dot(left, right.T, preferred_element_type=jnp.float32)
    dist = left_sq[:, None] + right_sq[None, :] - 2.0 * cross
    return (AMPLITUDE * jnp.exp(-GAMMA * dist)).astype(jnp.bfloat16)


def reference(embedding, direction, residual, solution, prior, plan, round_index):
    blocks = embedding.reshape(BLOCKS, ROWS, D)
    squares = jnp.sum(jnp.square(embedding.astype(jnp.float32)), axis=1).reshape(BLOCKS, ROWS)
    dir_low = direction.astype(jnp.bfloat16).reshape(BLOCKS, ROWS, PROBES)
    rounds_sum = jnp.zeros((NPTS, PROBES), jnp.float32)
    for step in range(ROUNDS):
        xor_mask = plan[round_index[0] + step]

        def one_block(index):
            partner = jnp.bitwise_xor(index, xor_mask).astype(jnp.int32)
            kern = kernel_block(blocks[index], squares[index], blocks[partner], squares[partner])
            return jnp.dot(kern, dir_low[partner], preferred_element_type=jnp.float32)

        term = lax.map(one_block, jnp.arange(BLOCKS, dtype=jnp.int32))
        rounds_sum = rounds_sum + term.reshape(NPTS, PROBES)
    image = prior + rounds_sum + NOISE * direction
    norm_now = jnp.sum(residual * residual, axis=0)
    curvature = jnp.sum(direction * image, axis=0)
    alpha = norm_now / curvature
    new_solution = solution + alpha * direction
    new_residual = residual - alpha * image
    norm_next = jnp.sum(new_residual * new_residual, axis=0)
    new_direction = new_residual + (norm_next / norm_now) * direction
    return new_solution, new_residual, new_direction
```

```python
import functools
import math

import jax
import jax.numpy as jnp
from jax import lax
from jax.experimental import pallas as pl
from jax.experimental.pallas import tpu as pltpu
from jax.sharding import PartitionSpec as P

ROUNDS = 3
GAMMA = 2.0
ROWS = 1024
DIM = 512
PROBES = 32
AXES = ("blk", "grp")
MESH = pl.DeviceIdType.MESH
VMEM = pl.BlockSpec(memory_space=pltpu.VMEM)
F32 = jnp.float32
BF16 = jnp.bfloat16
TALL = ROWS + 2 * PROBES
TILE = 256
CORE = 8
SCALE = -GAMMA * math.log2(math.e)
LOSS = 1e-2


def params(collective_id=None):
    return pltpu.CompilerParams(
        collective_id=collective_id,
        has_side_effects=collective_id is not None,
        vmem_limit_bytes=40 * 2**20,
    )


def prepare_kernel(x_ref, d_ref, both_ref, xt_ref, sq_ref, send_sem, recv_sem):
    blk, grp = lax.axis_index("blk"), lax.axis_index("grp")
    other = (blk ^ 1, grp)
    barrier = pltpu.get_barrier_semaphore()
    pl.semaphore_signal(barrier, inc=1, device_id=other, device_id_type=MESH)
    both_ref[0, :ROWS] = x_ref[...]
    low = d_ref[...].astype(BF16)
    both_ref[0, ROWS : ROWS + PROBES] = low[:, :DIM]
    both_ref[0, ROWS + PROBES :] = low[:, DIM:]
    pl.semaphore_wait(barrier, 1)
    copy = pltpu.make_async_remote_copy(
        src_ref=both_ref.at[0],
        dst_ref=both_ref.at[1],
        send_sem=send_sem,
        recv_sem=recv_sem,
        device_id=other,
        device_id_type=MESH,
    )
    copy.start()
    xt = x_ref[...].T
    xt_ref[...] = xt
    wide = xt.astype(F32)
    sq_ref[...] = jnp.sum(wide * wide, axis=0, keepdims=True)
    copy.wait()


def prepare(embedding, dir_t):
    return pl.pallas_call(
        prepare_kernel,
        out_shape=(
            jax.ShapeDtypeStruct((2, TALL, DIM), BF16),
            jax.ShapeDtypeStruct((DIM, ROWS), BF16),
            jax.ShapeDtypeStruct((1, ROWS), F32),
        ),
        in_specs=[VMEM] * 2,
        out_specs=(VMEM,) * 3,
        scratch_shapes=[pltpu.SemaphoreType.DMA, pltpu.SemaphoreType.DMA],
        compiler_params=params(1),
        name="prepare",
    )(embedding, dir_t)


def product_kernel(xt_ref, sq_ref, y_ref, acc_ref, out_ref):
    total = acc_ref[...]
    for tile in range(ROWS // TILE):
        part = y_ref[tile * TILE : (tile + 1) * TILE, :]
        wide = part.astype(F32)
        part_sq = jnp.sum(wide * wide, axis=1, keepdims=True)
        cross = jnp.dot(part, xt_ref[...], preferred_element_type=F32)
        dist = part_sq + sq_ref[...] - 2.0 * cross
        kern = jnp.exp2(SCALE * dist + 1.0).astype(BF16)
        half, column = divmod(tile * TILE, DIM)
        row = ROWS + half * PROBES
        probe = y_ref[row : row + PROBES, column : column + TILE]
        total = total + jnp.dot(probe, kern, preferred_element_type=F32)
    out_ref[...] = total


def product(xt, sq, partner, acc):
    return pl.pallas_call(
        product_kernel,
        out_shape=jax.ShapeDtypeStruct((PROBES, ROWS), F32),
        in_specs=[VMEM] * 4,
        out_specs=VMEM,
        compiler_params=params(),
        name="product",
    )(xt, sq, partner, acc)


def tree(ref):
    v = ref[...]
    while v.shape[0] > 1:
        half = v.shape[0] // 2
        v = v[:half] + v[half:]
    return v[0]


def exchange(slots, send_sem, recv_sem, place):
    count = slots.shape[0]
    for k in range(1, count):
        pltpu.make_async_remote_copy(
            src_ref=slots.at[0],
            dst_ref=slots.at[k],
            send_sem=send_sem,
            recv_sem=recv_sem,
            device_id=place(k),
            device_id_type=MESH,
        ).start()
    whole = pltpu.make_async_remote_copy(
        src_ref=slots.at[pl.ds(1, count - 1)],
        dst_ref=slots.at[pl.ds(1, count - 1)],
        send_sem=send_sem,
        recv_sem=recv_sem,
        device_id=place(1),
        device_id_type=MESH,
    )
    whole.wait_recv()
    return whole


def finish_kernel(
    d_ref, r_ref, s_ref, p_ref, acc_ref, ns_ref, nr_ref, nd_ref, bad_ref,
    near, far, near_send, near_recv, far_send, far_recv,
):
    blk, grp = lax.axis_index("blk"), lax.axis_index("grp")

    def near_place(k):
        return (blk ^ (k >> 3), grp ^ (k & 7))

    def far_place(k):
        return (blk ^ (k << 1), grp)

    barrier = pltpu.get_barrier_semaphore()
    for k in range(1, 16):
        pl.semaphore_signal(barrier, inc=1, device_id=near_place(k), device_id_type=MESH)
        pl.semaphore_signal(barrier, inc=1, device_id=far_place(k), device_id_type=MESH)
    d, r = d_ref[...], r_ref[...]
    image = p_ref[...] + acc_ref[...] + d
    columns = [
        jnp.sum(a * b, axis=1, keepdims=True)
        for a, b in ((r, r), (d, image), (r, image), (image, image))
    ]
    lane = lax.broadcasted_iota(jnp.int32, (8, 128), 1)
    packed = jnp.zeros((8, 128), F32)
    for q, column in enumerate(columns):
        for g in range(4):
            packed = jnp.where(lane == q * 4 + g, column[g * 8 : g * 8 + 8], packed)
    near[0] = packed
    pl.semaphore_wait(barrier, 30)
    first = exchange(near, near_send, near_recv, near_place)
    far[0] = tree(near)
    second = exchange(far, far_send, far_recv, far_place)
    total = tree(far)
    norm, curv, cross, square = (
        jnp.concatenate([total[:, q * 4 + g : q * 4 + g + 1] for g in range(4)], axis=0)
        for q in range(4)
    )
    alpha = norm / curv
    ns_ref[...] = s_ref[...] + alpha * d
    new_residual = r - alpha * image
    nr_ref[...] = new_residual
    twice, quad = 2.0 * alpha * cross, alpha * alpha * square
    following = norm - twice + quad
    good = following >= LOSS * (norm + jnp.abs(twice) + quad)
    good = jnp.logical_and(good, following < 3e38)
    nd_ref[...] = new_residual + (following / norm) * d
    bad = jnp.where(good, 0.0, 1.0)
    bad_ref[0, 0] = jnp.max(bad)
    bad_ref[0, 1] = 0.0
    first.wait_send()
    second.wait_send()


def finish(dir_t, res_t, sol_t, prior_t, acc):
    shape = jax.ShapeDtypeStruct((PROBES, ROWS), F32)
    return pl.pallas_call(
        finish_kernel,
        out_shape=(shape, shape, shape, jax.ShapeDtypeStruct((1, 2), F32)),
        in_specs=[VMEM] * 5,
        out_specs=(VMEM, VMEM, VMEM, pl.BlockSpec(memory_space=pltpu.SMEM)),
        scratch_shapes=[pltpu.VMEM((16, 8, 128), F32)] * 2 + [pltpu.SemaphoreType.DMA] * 4,
        compiler_params=params(2),
        name="finish",
    )(dir_t, res_t, sol_t, prior_t, acc)


def move_branches(count):
    def branch(chips):
        if chips == 0:
            return lambda block: block
        mask = (chips >> 3) << 4 | (chips & 7)
        route = [(i, i ^ mask) for i in range(count)]
        return lambda block: lax.ppermute(block, AXES, route)

    return [branch(chips) for chips in range(count // 2)]


def local(embedding, direction, residual, solution, prior, plan, round_index):
    count = lax.axis_size(AXES)
    branches = move_branches(count)
    dir_t, res_t = direction.T, residual.T
    both, xt, sq = prepare(embedding, dir_t)
    masks = lax.dynamic_slice(plan, (round_index[0],), (ROUNDS,))

    def one_round(step, acc):
        mask = masks[step]
        core = jnp.bitwise_and(mask >> 3, 1)
        chips = jnp.bitwise_or((mask >> 4) << 3, jnp.bitwise_and(mask, 7))
        block = lax.dynamic_index_in_dim(both, core, 0, keepdims=False)
        partner = lax.switch(chips, branches, block)
        return product(xt, sq, partner, acc)

    acc = lax.fori_loop(0, ROUNDS, one_round, jnp.zeros((PROBES, ROWS), F32))
    new_sol, new_res, new_dir, bad = finish(dir_t, res_t, solution.T, prior.T, acc)

    def again(new_dir):
        norm = lax.psum(jnp.sum(res_t * res_t, axis=1, keepdims=True), AXES)
        following = lax.psum(jnp.sum(new_res * new_res, axis=1, keepdims=True), AXES)
        return new_res + following / norm * dir_t

    new_dir = lax.cond(bad[0, 0] > 0, again, lambda v: v, new_dir)
    return new_sol.T, new_res.T, new_dir.T


def solution(mesh):
    rows = P(AXES, None)
    return jax.shard_map(
        local,
        mesh=mesh,
        in_specs=(rows,) * 5 + (P(), P()),
        out_specs=(rows,) * 3,
        check_vma=False,
    )
```

```python
import functools
import math

import jax
import jax.numpy as jnp
from jax import lax
from jax.experimental import pallas as pl
from jax.experimental.pallas import tpu as pltpu
from jax.sharding import PartitionSpec as P


ROUNDS = 3
GAMMA = 2.0
ROWS = 1024
DIM = 512
PROBES = 32
DEEP = 8
AXES = ("blk", "grp")
MESH = pl.DeviceIdType.MESH
VMEM = pl.BlockSpec(memory_space=pltpu.VMEM)
ANY = pl.BlockSpec(memory_space=pl.ANY)
F32 = jnp.float32
BF16 = jnp.bfloat16
TALL = DIM + PROBES
PART = 352
STARTS = (0, 336, 672)
PIECE = PART // 2
SCALE = -GAMMA * math.log2(math.e)
LOSS = 1e-2


def params(collective_id=None):
    return pltpu.CompilerParams(
        collective_id=collective_id,
        has_side_effects=collective_id is not None,
        vmem_limit_bytes=40 * 2**20,
    )


def prepare_kernel(x_ref, d_ref, out_ref):
    out_ref[:DIM] = x_ref[...].T
    out_ref[DIM:] = d_ref[...].astype(BF16)


def prepare(embedding, dir_t):
    return pl.pallas_call(
        prepare_kernel,
        out_shape=jax.ShapeDtypeStruct((TALL, ROWS), BF16),
        in_specs=[VMEM] * 2,
        out_specs=VMEM,
        compiler_params=params(),
        name="prepare",
    )(embedding, dir_t)


def move_kernel(
    rest, part_ref, block_ref, ring_ref, b_ref,
    own_sem, b_send, b_recv, right_send, right_recv, left_send, left_recv,
):
    blk, grp = lax.axis_index("blk"), lax.axis_index("grp")
    z = lax.rem(lax.div(blk, 2), DEEP)
    base = blk - 2 * z
    right = (base + 2 * lax.rem(z + 1, DEEP), grp)
    left = (base + 2 * lax.rem(z + DEEP - 1, DEEP), grp)
    other = (blk ^ ((rest >> 4) << 4 | (rest >> 3) & 1), grp ^ (rest & 7))
    barrier = pltpu.get_barrier_semaphore()
    greeted = [right, left] + ([other] if rest else [])
    for device in greeted:
        pl.semaphore_signal(barrier, inc=1, device_id=device, device_id_type=MESH)
    own = pltpu.make_async_copy(part_ref, ring_ref.at[0], own_sem)
    own.start()
    pl.semaphore_wait(barrier, len(greeted))

    def hop(to, step, piece, sends, recvs, sign):
        rows = pl.ds(piece * PIECE, PIECE)
        source = (sign * (step - 1)) % DEEP
        target = (sign * step) % DEEP
        src = part_ref.at[rows] if step == 1 else ring_ref.at[source, rows]
        return pltpu.make_async_remote_copy(
            src_ref=src,
            dst_ref=ring_ref.at[target, rows],
            send_sem=sends.at[step - 1, piece],
            recv_sem=recvs.at[step - 1, piece],
            device_id=to,
            device_id_type=MESH,
        )

    def rightward(step, piece):
        return hop(right, step, piece, right_send, right_recv, 1)

    def leftward(step, piece):
        return hop(left, step, piece, left_send, left_recv, -1)

    order = [
        (way, step, piece)
        for step in range(1, 5)
        for piece in range(2)
        for way in (rightward, leftward)
        if step < 4 or (way is rightward) == (piece == 0)
    ]
    for way, step, piece in order[:4]:
        way(step, piece).start()
    if rest:
        direct = pltpu.make_async_remote_copy(
            src_ref=block_ref,
            dst_ref=b_ref,
            send_sem=b_send,
            recv_sem=b_recv,
            device_id=other,
            device_id_type=MESH,
        )
    else:
        direct = pltpu.make_async_copy(block_ref, b_ref, b_send)
    direct.start()
    for way, step, piece in order[4:]:
        way(step - 1, piece).wait_recv()
        way(step, piece).start()
    for way, step, piece in order:
        way(step, piece).wait_send()
    for way, step, piece in order:
        if step == 4 or (way is rightward) != (piece == 0) and step == 3:
            way(step, piece).wait_recv()
    direct.wait()
    own.wait()


def move(rest, part, block):
    pair = pltpu.SemaphoreType.DMA((4, 2))
    one = pltpu.SemaphoreType.DMA
    return pl.pallas_call(
        functools.partial(move_kernel, rest),
        out_shape=(
            jax.ShapeDtypeStruct((DEEP, PART, DIM), BF16),
            jax.ShapeDtypeStruct((TALL, ROWS), BF16),
        ),
        in_specs=[ANY] * 2,
        out_specs=(ANY, ANY),
        scratch_shapes=[one, one, one, pair, pair, pair, pair],
        compiler_params=params(2 + rest),
        name=f"move_{rest}",
    )(part, block)


def move_by(rest, part, block):
    def branch(high, low):
        return lambda a, b: move(high * 8 + low, a, b)

    def inner(high):
        return lambda a, b: lax.switch(
            jnp.bitwise_and(rest, 7), [branch(high, low) for low in range(8)], a, b
        )

    return lax.switch(rest >> 3, [inner(high) for high in range(4)], part, block)


def term_kernel(slot_ref, first_ref, second_ref, third_ref, b_ref, out_ref, rows_ref):
    del slot_ref
    bt = b_ref[:DIM]
    wide = bt.astype(F32)
    b_sq = jnp.sum(wide * wide, axis=0, keepdims=True)
    probes = b_ref[DIM:].astype(F32).T.astype(BF16)
    ends = STARTS[1:] + (ROWS,)
    for ref, start, end in zip((first_ref, second_ref, third_ref), STARTS, ends):
        a = ref[0, : end - start]
        a_wide = a.astype(F32)
        a_sq = jnp.sum(a_wide * a_wide, axis=1, keepdims=True)
        cross = jnp.dot(a, bt, preferred_element_type=F32)
        dist = a_sq + b_sq - 2.0 * cross
        kern = jnp.exp2(SCALE * dist + 1.0).astype(BF16)
        rows_ref[start:end, :PROBES] = jnp.dot(kern, probes, preferred_element_type=F32)
    out_ref[...] = rows_ref[...].T[:PROBES]


def term(slot, parts, block):
    part_spec = pl.BlockSpec((1, PART, DIM), lambda i, slot: (slot[0], 0, 0))
    return pl.pallas_call(
        term_kernel,
        out_shape=jax.ShapeDtypeStruct((PROBES, ROWS), F32),
        grid_spec=pltpu.PrefetchScalarGridSpec(
            num_scalar_prefetch=1,
            grid=(1,),
            in_specs=[part_spec] * 3 + [pl.BlockSpec((TALL, ROWS), lambda i, slot: (0, 0))],
            out_specs=pl.BlockSpec((PROBES, ROWS), lambda i, slot: (0, 0)),
            scratch_shapes=[pltpu.VMEM((ROWS, 128), F32)],
        ),
        compiler_params=params(),
        name="term",
    )(slot, *parts, block)


def tree(ref):
    v = ref[...]
    while v.shape[0] > 1:
        half = v.shape[0] // 2
        v = v[:half] + v[half:]
    return v[0]


def exchange(source, slots, send_sem, recv_sem, place):
    count = slots.shape[0]
    for k in range(1, count):
        pltpu.make_async_remote_copy(
            src_ref=source(k),
            dst_ref=slots.at[k],
            send_sem=send_sem,
            recv_sem=recv_sem,
            device_id=place(k),
            device_id_type=MESH,
        ).start()
    whole = pltpu.make_async_remote_copy(
        src_ref=slots.at[pl.ds(1, count - 1)],
        dst_ref=slots.at[pl.ds(1, count - 1)],
        send_sem=send_sem,
        recv_sem=recv_sem,
        device_id=place(1),
        device_id_type=MESH,
    )
    whole.wait_recv()
    return whole


def finish_kernel(
    depth_ref, d_ref, r_ref, s_ref, p_ref, t0_ref, t1_ref, t2_ref,
    ns_ref, nr_ref, nd_ref, bad_ref,
    sent, back, near, far, back_send, back_recv, near_send, near_recv, far_send, far_recv,
):
    blk, grp = lax.axis_index("blk"), lax.axis_index("grp")

    def near_place(k):
        return (blk ^ (k >> 3), grp ^ (k & 7))

    def far_place(k):
        return (blk ^ (k << 1), grp)

    barrier = pltpu.get_barrier_semaphore()
    for k in range(1, 16):
        pl.semaphore_signal(barrier, inc=1, device_id=near_place(k), device_id_type=MESH)
        pl.semaphore_signal(barrier, inc=1, device_id=far_place(k), device_id_type=MESH)
    terms = (t0_ref[...], t1_ref[...], t2_ref[...])

    def meant_for(k):
        return sum(jnp.where(depth_ref[s] == k, terms[s], 0.0) for s in range(ROUNDS))

    for k in range(1, DEEP):
        sent[k] = meant_for(k).astype(BF16)
    pl.semaphore_wait(barrier, 30)
    zeroth = exchange(lambda k: sent.at[k], back, back_send, back_recv, far_place)
    d, r = d_ref[...], r_ref[...]
    image = p_ref[...] + d + meant_for(0)
    for k in range(1, DEEP):
        image = image + back[k].astype(F32)
    columns = [
        jnp.sum(a * b, axis=1, keepdims=True)
        for a, b in ((r, r), (d, image), (r, image), (image, image))
    ]
    lane = lax.broadcasted_iota(jnp.int32, (8, 128), 1)
    packed = jnp.zeros((8, 128), F32)
    for q, column in enumerate(columns):
        for g in range(4):
            packed = jnp.where(lane == q * 4 + g, column[g * 8 : g * 8 + 8], packed)
    near[0] = packed
    first = exchange(lambda k: near.at[0], near, near_send, near_recv, near_place)
    far[0] = tree(near)
    second = exchange(lambda k: far.at[0], far, far_send, far_recv, far_place)
    total = tree(far)
    norm, curv, cross, square = (
        jnp.concatenate([total[:, q * 4 + g : q * 4 + g + 1] for g in range(4)], axis=0)
        for q in range(4)
    )
    alpha = norm / curv
    ns_ref[...] = s_ref[...] + alpha * d
    new_residual = r - alpha * image
    nr_ref[...] = new_residual
    twice, quad = 2.0 * alpha * cross, alpha * alpha * square
    following = norm - twice + quad
    good = following >= LOSS * (norm + jnp.abs(twice) + quad)
    good = jnp.logical_and(good, following < 3e38)
    nd_ref[...] = new_residual + (following / norm) * d
    bad = jnp.where(good, 0.0, 1.0)
    bad_ref[0, 0] = jnp.max(bad)
    bad_ref[0, 1] = 0.0
    zeroth.wait_send()
    first.wait_send()
    second.wait_send()


def finish(depths, dir_t, res_t, sol_t, prior_t, terms):
    shape = jax.ShapeDtypeStruct((PROBES, ROWS), F32)
    smem = pl.BlockSpec(memory_space=pltpu.SMEM)
    return pl.pallas_call(
        finish_kernel,
        out_shape=(shape, shape, shape, jax.ShapeDtypeStruct((1, 2), F32)),
        in_specs=[smem] + [VMEM] * 7,
        out_specs=(VMEM, VMEM, VMEM, smem),
        scratch_shapes=[pltpu.VMEM((DEEP, PROBES, ROWS), BF16)] * 2
        + [pltpu.VMEM((16, 8, 128), F32)] * 2
        + [pltpu.SemaphoreType.DMA] * 6,
        compiler_params=params(1),
        name="finish",
    )(depths, dir_t, res_t, sol_t, prior_t, *terms)


def local(embedding, direction, residual, solution, prior, plan, round_index):
    dir_t, res_t = direction.T, residual.T
    masks = lax.dynamic_slice(plan, (round_index[0],), (ROUNDS,))
    depths = jnp.bitwise_and(masks >> 4, DEEP - 1)
    rests = jnp.bitwise_or((masks >> 7) << 4, jnp.bitwise_and(masks, 15))
    z = jnp.bitwise_and(lax.axis_index("blk") >> 1, DEEP - 1)
    slots = jnp.bitwise_and(z - jnp.bitwise_xor(z, depths), DEEP - 1).astype(jnp.int32)
    block = prepare(embedding, dir_t)
    parts, blocks = [], []
    for step in range(ROUNDS):
        part, arrived = move_by(rests[step], embedding[STARTS[step] : STARTS[step] + PART], block)
        parts.append(part)
        blocks.append(arrived)
    terms = [term(slots[step : step + 1], parts, blocks[step]) for step in range(ROUNDS)]
    new_sol, new_res, new_dir, bad = finish(depths, dir_t, res_t, solution.T, prior.T, terms)

    def again(new_dir):
        norm = lax.psum(jnp.sum(res_t * res_t, axis=1, keepdims=True), AXES)
        following = lax.psum(jnp.sum(new_res * new_res, axis=1, keepdims=True), AXES)
        return new_res + following / norm * dir_t

    new_dir = lax.cond(bad[0, 0] > 0, again, lambda v: v, new_dir)
    return new_sol.T, new_res.T, new_dir.T


def solution(mesh):
    rows = P(AXES, None)
    return jax.shard_map(
        local,
        mesh=mesh,
        in_specs=(rows,) * 5 + (P(), P()),
        out_specs=(rows,) * 3,
        check_vma=False,
    )
```

```python
import functools
import math

import jax
import jax.numpy as jnp
from jax import lax
from jax.experimental import pallas as pl
from jax.experimental.pallas import tpu as pltpu
from jax.sharding import PartitionSpec as P


ROUNDS = 3
GAMMA = 2.0
ROWS = 1024
DIM = 512
PROBES = 32
DEEP = 8
AXES = ("blk", "grp")
MESH = pl.DeviceIdType.MESH
VMEM = pl.BlockSpec(memory_space=pltpu.VMEM)
SMEM = pl.BlockSpec(memory_space=pltpu.SMEM)
ANY = pl.BlockSpec(memory_space=pl.ANY)
F32 = jnp.float32
BF16 = jnp.bfloat16
TALL = DIM + PROBES
PART = 352
STARTS = (0, 336, 672)
ENDS = (336, 672, 1024)
PIECES = ((0, 96), (96, 80), (176, 96), (272, 80))
HALF = len(PIECES) // 2
CUTS = (0, 256, 640, 1024)
SCALE = -GAMMA * math.log2(math.e)
LOSS = 1e-2


def params(collective_id=None):
    return pltpu.CompilerParams(
        collective_id=collective_id,
        has_side_effects=collective_id is not None,
        vmem_limit_bytes=40 * 2**20,
    )


def prepare_kernel(plan_ref, first_ref, x_ref, d_ref, out_ref, p0_ref, p1_ref, p2_ref, mask_ref):
    for step in range(ROUNDS):
        mask = plan_ref[first_ref[0] + step]
        mask_ref[0, step] = ((mask >> 7) << 4) | (mask & 15)
        mask_ref[1, step] = (mask >> 4) & (DEEP - 1)
    out_ref[:DIM] = x_ref[...].T
    out_ref[DIM:] = d_ref[...].astype(BF16)
    for ref, start in zip((p0_ref, p1_ref, p2_ref), STARTS):
        ref[...] = x_ref[start : start + PART]


def prepare(plan, first, embedding, dir_t):
    part = jax.ShapeDtypeStruct((PART, DIM), BF16)
    return pl.pallas_call(
        prepare_kernel,
        out_shape=(
            jax.ShapeDtypeStruct((TALL, ROWS), BF16),
            part,
            part,
            part,
            jax.ShapeDtypeStruct((2, ROUNDS), jnp.int32),
        ),
        in_specs=[SMEM] * 2 + [VMEM] * 2,
        out_specs=(VMEM,) * 4 + (SMEM,),
        compiler_params=params(),
        name="prepare",
    )(plan, first, embedding, dir_t)


def move_kernel(
    rest, part_ref, block_ref, ring_ref, b_ref,
    own_sem, b_send, b_recv, right_send, right_recv, left_send, left_recv,
):
    blk, grp = lax.axis_index("blk"), lax.axis_index("grp")
    z = lax.rem(lax.div(blk, 2), DEEP)
    base = blk - 2 * z
    right = (base + 2 * lax.rem(z + 1, DEEP), grp)
    left = (base + 2 * lax.rem(z + DEEP - 1, DEEP), grp)
    other = (blk ^ ((rest >> 4) << 4 | (rest >> 3) & 1), grp ^ (rest & 7))
    barrier = pltpu.get_barrier_semaphore()
    greeted = [right, left] + ([other] if rest else [])
    for device in greeted:
        pl.semaphore_signal(barrier, inc=1, device_id=device, device_id_type=MESH)
    own = pltpu.make_async_copy(part_ref, ring_ref.at[0], own_sem)
    own.start()
    pl.semaphore_wait(barrier, len(greeted))

    def hop(to, step, piece, sends, recvs, sign):
        rows = pl.ds(*PIECES[piece])
        source = (sign * (step - 1)) % DEEP
        target = (sign * step) % DEEP
        src = part_ref.at[rows] if step == 1 else ring_ref.at[source, rows]
        return pltpu.make_async_remote_copy(
            src_ref=src,
            dst_ref=ring_ref.at[target, rows],
            send_sem=sends.at[step - 1, piece],
            recv_sem=recvs.at[step - 1, piece],
            device_id=to,
            device_id_type=MESH,
        )

    def rightward(step, piece):
        return hop(right, step, piece, right_send, right_recv, 1)

    def leftward(step, piece):
        return hop(left, step, piece, left_send, left_recv, -1)

    order = [
        (way, step, piece)
        for step in range(1, 5)
        for piece in range(len(PIECES))
        for way in (rightward, leftward)
        if step < 4 or (way is rightward) == (piece < HALF)
    ]
    for way, step, piece in order:
        if step == 1:
            way(step, piece).start()
    if rest:
        direct = pltpu.make_async_remote_copy(
            src_ref=block_ref,
            dst_ref=b_ref,
            send_sem=b_send,
            recv_sem=b_recv,
            device_id=other,
            device_id_type=MESH,
        )
    else:
        direct = pltpu.make_async_copy(block_ref, b_ref, b_send)
    direct.start()
    for way, step, piece in order:
        if step > 1:
            way(step - 1, piece).wait_recv()
            way(step, piece).start()
    for way, step, piece in order:
        way(step, piece).wait_send()
    for way, step, piece in order:
        if step == 4 or step == 3 and (way is rightward) != (piece < HALF):
            way(step, piece).wait_recv()
    direct.wait()
    own.wait()


def move(rest, part, block):
    pair = pltpu.SemaphoreType.DMA((4, len(PIECES)))
    one = pltpu.SemaphoreType.DMA
    return pl.pallas_call(
        functools.partial(move_kernel, rest),
        out_shape=(
            jax.ShapeDtypeStruct((DEEP, PART, DIM), BF16),
            jax.ShapeDtypeStruct((TALL, ROWS), BF16),
        ),
        in_specs=[ANY] * 2,
        out_specs=(ANY, ANY),
        scratch_shapes=[one, one, one, pair, pair, pair, pair],
        compiler_params=params(2 + rest),
        name=f"move_{rest}",
    )(part, block)


def move_by(rest, part, block):
    def branch(high, low):
        return lambda a, b: move(high * 8 + low, a, b)

    def inner(high):
        return lambda a, b: lax.switch(
            jnp.bitwise_and(rest, 7), [branch(high, low) for low in range(8)], a, b
        )

    return lax.switch(rest >> 3, [inner(high) for high in range(4)], part, block)


def tree(ref):
    v = ref[...]
    while v.shape[0] > 1:
        half = v.shape[0] // 2
        v = v[:half] + v[half:]
    return v[0]


def exchange(slots, send_sem, recv_sem, place):
    count = slots.shape[0]
    for k in range(1, count):
        pltpu.make_async_remote_copy(
            src_ref=slots.at[0],
            dst_ref=slots.at[k],
            send_sem=send_sem,
            recv_sem=recv_sem,
            device_id=place(k),
            device_id_type=MESH,
        ).start()
    whole = pltpu.make_async_remote_copy(
        src_ref=slots.at[pl.ds(1, count - 1)],
        dst_ref=slots.at[pl.ds(1, count - 1)],
        send_sem=send_sem,
        recv_sem=recv_sem,
        device_id=place(1),
        device_id_type=MESH,
    )
    whole.wait_recv()
    return whole


def finish_kernel(
    mask_ref, d_ref, r_ref, p_ref, g0_ref, g1_ref, g2_ref, b0_ref, b1_ref, b2_ref,
    image_ref, alpha_ref, beta_ref, bad_ref,
    g0, g1, g2, b0, b1, b2, terms, sent, back, near, far,
    load_sem, back_send, back_recv, near_send, near_recv, far_send, far_recv,
):
    blk, grp = lax.axis_index("blk"), lax.axis_index("grp")
    z = lax.rem(lax.div(blk, 2), DEEP)

    def near_place(k):
        return (blk ^ ((k >> 3) << 4), grp ^ (k & 7))

    def far_place(k):
        return (blk ^ k, grp)

    barrier = pltpu.get_barrier_semaphore()
    for k in range(1, 16):
        pl.semaphore_signal(barrier, inc=1, device_id=near_place(k), device_id_type=MESH)
        pl.semaphore_signal(barrier, inc=1, device_id=far_place(k), device_id_type=MESH)
    loads = [
        pltpu.make_async_copy(src, dst, load_sem.at[i])
        for i, (src, dst) in enumerate(
            ((b0_ref, b0), (g0_ref, g0), (b1_ref, b1), (b2_ref, b2), (g1_ref, g1), (g2_ref, g2))
        )
    ]
    for load in loads:
        load.start()
    awaited = {(0, 0): (0, 1), (0, 1): (2,), (0, 2): (3,), (1, 0): (4,), (2, 0): (5,)}
    depths = [mask_ref[1, s] for s in range(ROUNDS)]
    right_sq, pieces = [], []
    for part, gathered in enumerate((g0, g1, g2)):
        start, end = STARTS[part], ENDS[part]
        for s, block in enumerate((b0, b1, b2)):
            for i in awaited.get((part, s), ()):
                loads[i].wait()
            if part == 0:
                wide = block[:DIM].astype(F32)
                right_sq.append(SCALE * jnp.sum(wide * wide, axis=0, keepdims=True))
            slot = (z - (z ^ depths[s])) & (DEEP - 1)
            a = gathered[slot, : end - start]
            wide = a.astype(F32)
            left_sq = SCALE * jnp.sum(wide * wide, axis=1, keepdims=True) + 1.0
            cross = jnp.dot(a, block[:DIM], preferred_element_type=F32)
            kern = jnp.exp2((left_sq + right_sq[s]) + (-2.0 * SCALE) * cross).astype(BF16)
            terms[s, :, start:end] = lax.dot_general(
                block[DIM:], kern, (((1,), (1,)), ((), ())), preferred_element_type=F32
            )
        columns = slice(CUTS[part], CUTS[part + 1])
        for k in range(1, DEEP):
            meant = sum(
                jnp.where(depths[s] == k, terms[s, :, columns], 0.0) for s in range(ROUNDS)
            )
            sent[k, :, columns] = meant.astype(BF16)
        if part == 0:
            pl.semaphore_wait(barrier, 30)
        lanes = pl.ds(CUTS[part], CUTS[part + 1] - CUTS[part])
        for k in range(1, DEEP):
            pltpu.make_async_remote_copy(
                src_ref=sent.at[k, :, lanes],
                dst_ref=back.at[k, :, lanes],
                send_sem=back_send.at[part],
                recv_sem=back_recv.at[part],
                device_id=far_place(2 * k),
                device_id_type=MESH,
            ).start()
        pieces.append(
            pltpu.make_async_remote_copy(
                src_ref=sent.at[pl.ds(1, DEEP - 1), :, lanes],
                dst_ref=back.at[pl.ds(1, DEEP - 1), :, lanes],
                send_sem=back_send.at[part],
                recv_sem=back_recv.at[part],
                device_id=far_place(2),
                device_id_type=MESH,
            )
        )
    columns = [0.0] * 4
    for part, piece in enumerate(pieces):
        piece.wait_recv()
        cut = slice(CUTS[part], CUTS[part + 1])
        d, r = d_ref[:, cut], r_ref[:, cut]
        image = p_ref[:, cut] + d
        for s in range(ROUNDS):
            image = image + jnp.where(depths[s] == 0, terms[s, :, cut], 0.0)
        for k in range(1, DEEP):
            image = image + back[k, :, cut].astype(F32)
        image_ref[:, cut] = image
        for q, (a, b) in enumerate(((r, r), (d, image), (r, image), (image, image))):
            columns[q] = columns[q] + jnp.sum(a * b, axis=1, keepdims=True)
    lane = lax.broadcasted_iota(jnp.int32, (8, 128), 1)
    packed = jnp.zeros((8, 128), F32)
    for q, column in enumerate(columns):
        for g in range(4):
            packed = jnp.where(lane == q * 4 + g, column[g * 8 : g * 8 + 8], packed)
    near[0] = packed
    first = exchange(near, near_send, near_recv, near_place)
    far[0] = tree(near)
    second = exchange(far, far_send, far_recv, far_place)
    total = tree(far)
    norm, curv, cross, square = (
        jnp.concatenate([total[:, q * 4 + g : q * 4 + g + 1] for g in range(4)], axis=0)
        for q in range(4)
    )
    alpha = norm / curv
    alpha_ref[...] = alpha
    twice, quad = 2.0 * alpha * cross, alpha * alpha * square
    following = norm - twice + quad
    good = following >= LOSS * (norm + jnp.abs(twice) + quad)
    good = jnp.logical_and(good, following < 3e38)
    beta_ref[...] = following / norm
    bad_ref[0, 0] = jnp.max(jnp.where(good, 0.0, 1.0))
    bad_ref[0, 1] = 0.0
    for piece in pieces:
        piece.wait_send()
    first.wait_send()
    second.wait_send()


def finish(masks, dir_t, res_t, prior_t, parts, blocks):
    column = jax.ShapeDtypeStruct((PROBES, 1), F32)
    dma = pltpu.SemaphoreType.DMA
    return pl.pallas_call(
        finish_kernel,
        out_shape=(
            jax.ShapeDtypeStruct((PROBES, ROWS), F32),
            column,
            column,
            jax.ShapeDtypeStruct((1, 2), F32),
        ),
        in_specs=[SMEM] + [VMEM] * 3 + [ANY] * 6,
        out_specs=(VMEM, VMEM, VMEM, SMEM),
        scratch_shapes=[pltpu.VMEM((DEEP, PART, DIM), BF16)] * 3
        + [pltpu.VMEM((TALL, ROWS), BF16)] * 3
        + [pltpu.VMEM((ROUNDS, PROBES, ROWS), F32)]
        + [pltpu.VMEM((DEEP, PROBES, ROWS), BF16)] * 2
        + [pltpu.VMEM((16, 8, 128), F32)] * 2
        + [dma((6,)), dma((3,)), dma((3,)), dma, dma, dma, dma],
        compiler_params=params(1),
        name="finish",
    )(masks, dir_t, res_t, prior_t, *parts, *blocks)


def result_kernel(d_ref, r_ref, s_ref, image_ref, alpha_ref, beta_ref, ns_ref, nr_ref, nd_ref):
    d, alpha = d_ref[...], alpha_ref[...]
    ns_ref[...] = s_ref[...] + alpha * d
    new_residual = r_ref[...] - alpha * image_ref[...]
    nr_ref[...] = new_residual
    nd_ref[...] = new_residual + beta_ref[...] * d


def result(*operands):
    shape = jax.ShapeDtypeStruct((PROBES, ROWS), F32)
    return pl.pallas_call(
        result_kernel,
        out_shape=(shape,) * 3,
        in_specs=[VMEM] * 6,
        out_specs=(VMEM,) * 3,
        compiler_params=params(),
        name="result",
    )(*operands)


def local(embedding, direction, residual, solution, prior, plan, round_index):
    dir_t, res_t = direction.T, residual.T
    block, *own, masks = prepare(plan, round_index, embedding, dir_t)
    parts, blocks = [], []
    for step in range(ROUNDS):
        part, arrived = move_by(masks[0, step], own[step], block)
        parts.append(part)
        blocks.append(arrived)
    image, alpha, beta, bad = finish(masks, dir_t, res_t, prior.T, parts, blocks)

    def again():
        new_res = res_t - alpha * image
        norm = lax.psum(jnp.sum(res_t * res_t, axis=1, keepdims=True), AXES)
        return lax.psum(jnp.sum(new_res * new_res, axis=1, keepdims=True), AXES) / norm

    beta = lax.cond(bad[0, 0] > 0, again, lambda: beta)
    results = result(dir_t, res_t, solution.T, image, alpha, beta)
    return tuple(out.T for out in results)


def solution(mesh):
    rows = P(AXES, None)
    return jax.shard_map(
        local,
        mesh=mesh,
        in_specs=(rows,) * 5 + (P(), P()),
        out_specs=(rows,) * 3,
        check_vma=False,
    )
```

```python
import functools
import math

import jax
import jax.numpy as jnp
from jax import lax
from jax.experimental import pallas as pl
from jax.experimental.pallas import tpu as pltpu
from jax.sharding import PartitionSpec as P


ROUNDS = 3
GAMMA = 2.0
ROWS = 1024
DIM = 512
PROBES = 32
DEEP = 8
AXES = ("blk", "grp")
MESH = pl.DeviceIdType.MESH
VMEM = pl.BlockSpec(memory_space=pltpu.VMEM)
SMEM = pl.BlockSpec(memory_space=pltpu.SMEM)
ANY = pl.BlockSpec(memory_space=pl.ANY)
F32 = jnp.float32
BF16 = jnp.bfloat16
TALL = DIM + PROBES
PART = 352
STARTS = (0, 336, 672)
PIECE = PART // 2
CUTS = (0, 256, 640, 1024)
SCALE = -GAMMA * math.log2(math.e)
LOSS = 1e-2


def params(collective_id=None):
    return pltpu.CompilerParams(
        collective_id=collective_id,
        has_side_effects=collective_id is not None,
        vmem_limit_bytes=40 * 2**20,
    )


def prepare_kernel(x_ref, d_ref, out_ref, p0_ref, p1_ref, p2_ref):
    out_ref[:DIM] = x_ref[...].T
    out_ref[DIM:] = d_ref[...].astype(BF16)
    for ref, start in zip((p0_ref, p1_ref, p2_ref), STARTS):
        ref[...] = x_ref[start : start + PART]


def prepare(embedding, dir_t):
    part = jax.ShapeDtypeStruct((PART, DIM), BF16)
    return pl.pallas_call(
        prepare_kernel,
        out_shape=(jax.ShapeDtypeStruct((TALL, ROWS), BF16), part, part, part),
        in_specs=[VMEM] * 2,
        out_specs=(VMEM,) * 4,
        compiler_params=params(),
        name="prepare",
    )(embedding, dir_t)


def move_kernel(
    rest, part_ref, block_ref, ring_ref, b_ref,
    own_sem, b_send, b_recv, right_send, right_recv, left_send, left_recv,
):
    blk, grp = lax.axis_index("blk"), lax.axis_index("grp")
    z = lax.rem(lax.div(blk, 2), DEEP)
    base = blk - 2 * z
    right = (base + 2 * lax.rem(z + 1, DEEP), grp)
    left = (base + 2 * lax.rem(z + DEEP - 1, DEEP), grp)
    other = (blk ^ ((rest >> 4) << 4 | (rest >> 3) & 1), grp ^ (rest & 7))
    barrier = pltpu.get_barrier_semaphore()
    greeted = [right, left] + ([other] if rest else [])
    for device in greeted:
        pl.semaphore_signal(barrier, inc=1, device_id=device, device_id_type=MESH)
    own = pltpu.make_async_copy(part_ref, ring_ref.at[0], own_sem)
    own.start()
    pl.semaphore_wait(barrier, len(greeted))

    def hop(to, step, piece, send, recvs, sign):
        rows = pl.ds(piece * PIECE, PIECE)
        source = lax.rem(DEEP + sign * (step - 1), DEEP)
        target = lax.rem(DEEP + sign * step, DEEP)
        return pltpu.make_async_remote_copy(
            src_ref=ring_ref.at[source, rows],
            dst_ref=ring_ref.at[target, rows],
            send_sem=send,
            recv_sem=recvs.at[step - 1, piece],
            device_id=to,
            device_id_type=MESH,
        )

    def rightward(step, piece, send=right_send.at[0]):
        return hop(right, step, piece, send, right_recv, 1)

    def leftward(step, piece, send=left_send.at[0]):
        return hop(left, step, piece, send, left_recv, -1)

    def begin(piece, carry):
        rightward(1, piece).start()
        leftward(1, piece).start()
        return carry

    def pass_on(index, carry):
        step, piece = lax.div(index, 2), lax.rem(index, 2)
        rightward(step - 1, piece).wait_recv()
        rightward(step, piece).start()
        leftward(step - 1, piece).wait_recv()
        leftward(step, piece).start()
        return carry

    own.wait()
    lax.fori_loop(0, 2, begin, 0)
    if rest:
        direct = pltpu.make_async_remote_copy(
            src_ref=block_ref,
            dst_ref=b_ref,
            send_sem=b_send,
            recv_sem=b_recv,
            device_id=other,
            device_id_type=MESH,
        )
    else:
        direct = pltpu.make_async_copy(block_ref, b_ref, b_send)
    direct.start()
    lax.fori_loop(4, 8, pass_on, 0)
    rightward(3, 0).wait_recv()
    last_right = rightward(4, 0, right_send.at[1])
    last_right.start()
    leftward(3, 1).wait_recv()
    last_left = leftward(4, 1, left_send.at[1])
    last_left.start()
    rightward(3, 1).wait_recv()
    leftward(3, 0).wait_recv()
    for send in (right_send, left_send):
        whole = ring_ref.at[pl.ds(0, 3)]
        pltpu.make_async_remote_copy(
            src_ref=whole,
            dst_ref=whole,
            send_sem=send.at[0],
            recv_sem=right_recv.at[0, 0],
            device_id=right,
            device_id_type=MESH,
        ).wait_send()
    last_right.wait()
    last_left.wait()
    direct.wait()


def move(rest, part, block):
    one = pltpu.SemaphoreType.DMA
    sends, recvs = one((2,)), one((4, 2))
    return pl.pallas_call(
        functools.partial(move_kernel, rest),
        out_shape=(
            jax.ShapeDtypeStruct((DEEP, PART, DIM), BF16),
            jax.ShapeDtypeStruct((TALL, ROWS), BF16),
        ),
        in_specs=[ANY] * 2,
        out_specs=(ANY, ANY),
        scratch_shapes=[one, one, one, sends, recvs, sends, recvs],
        compiler_params=params(2 + rest),
        name=f"move_{rest}",
    )(part, block)


def move_by(rest, part, block):
    return lax.switch(rest, [functools.partial(move, k) for k in range(32)], part, block)


def tree(ref):
    v = ref[...]
    while v.shape[0] > 1:
        half = v.shape[0] // 2
        v = v[:half] + v[half:]
    return v[0]


def exchange(slots, send_sem, recv_sem, place):
    count = slots.shape[0]

    def send(k, carry):
        pltpu.make_async_remote_copy(
            src_ref=slots.at[0],
            dst_ref=slots.at[k],
            send_sem=send_sem,
            recv_sem=recv_sem,
            device_id=place(k),
            device_id_type=MESH,
        ).start()
        return carry

    lax.fori_loop(1, count, send, 0)
    whole = pltpu.make_async_remote_copy(
        src_ref=slots.at[pl.ds(1, count - 1)],
        dst_ref=slots.at[pl.ds(1, count - 1)],
        send_sem=send_sem,
        recv_sem=recv_sem,
        device_id=place(1),
        device_id_type=MESH,
    )
    whole.wait_recv()
    return whole


def finish_kernel(
    depth_ref, d_ref, r_ref, p_ref, g0_ref, g1_ref, g2_ref, b0_ref, b1_ref, b2_ref,
    image_ref, alpha_ref, beta_ref, bad_ref,
    g0, g1, g2, blocks, right_sq, terms, sent, back, near, far,
    part_sem, block_sem, back_send, back_recv, near_send, near_recv, far_send, far_recv,
):
    blk, grp = lax.axis_index("blk"), lax.axis_index("grp")
    z = lax.rem(lax.div(blk, 2), DEEP)

    def near_place(k):
        return (blk ^ ((k >> 3) << 4), grp ^ (k & 7))

    def far_place(k):
        return (blk ^ k, grp)

    barrier = pltpu.get_barrier_semaphore()

    def greet(k, carry):
        pl.semaphore_signal(barrier, inc=1, device_id=near_place(k), device_id_type=MESH)
        pl.semaphore_signal(barrier, inc=1, device_id=far_place(k), device_id_type=MESH)
        return carry

    lax.fori_loop(1, 16, greet, 0)

    def load_block(s):
        return pltpu.make_async_copy((b0_ref, b1_ref, b2_ref)[s], blocks.at[s], block_sem.at[s])

    def load_part(part):
        refs = ((g0_ref, g0), (g1_ref, g1), (g2_ref, g2))
        return pltpu.make_async_copy(*refs[part], part_sem.at[part])

    load_block(0).start()
    load_part(0).start()
    for s in range(1, ROUNDS):
        load_block(s).start()
    for part in range(1, ROUNDS):
        load_part(part).start()
    depths = [depth_ref[s] for s in range(ROUNDS)]
    pieces = []
    for part, gathered in enumerate((g0, g1, g2)):
        load_part(part).wait()

        def one_term(s, carry, part=part, gathered=gathered):
            if part == 0:
                pltpu.make_async_copy(b0_ref, blocks.at[s], block_sem.at[s]).wait()
                wide = blocks[s, :DIM].astype(F32)
                right_sq[s] = SCALE * jnp.sum(wide * wide, axis=0, keepdims=True)
            slot = (z - (z ^ depth_ref[s])) & (DEEP - 1)
            a = gathered[slot]
            wide = a.astype(F32)
            left_sq = SCALE * jnp.sum(wide * wide, axis=1, keepdims=True) + 1.0
            cross = jnp.dot(a, blocks[s, :DIM], preferred_element_type=F32)
            kern = jnp.exp2((left_sq + right_sq[s]) + (-2.0 * SCALE) * cross).astype(BF16)
            terms[s, :, STARTS[part] : STARTS[part] + PART] = lax.dot_general(
                blocks[s, DIM:], kern, (((1,), (1,)), ((), ())), preferred_element_type=F32
            )
            return carry

        lax.fori_loop(0, ROUNDS, one_term, 0)
        columns = slice(CUTS[part], CUTS[part + 1])
        lanes = pl.ds(CUTS[part], CUTS[part + 1] - CUTS[part])
        if part == 0:
            pl.semaphore_wait(barrier, 30)

        def give_back(k, carry, part=part, columns=columns, lanes=lanes):
            meant = sum(
                jnp.where(depths[s] == k, terms[s, :, columns], 0.0) for s in range(ROUNDS)
            )
            sent[k, :, columns] = meant.astype(BF16)
            pltpu.make_async_remote_copy(
                src_ref=sent.at[k, :, lanes],
                dst_ref=back.at[k, :, lanes],
                send_sem=back_send.at[part],
                recv_sem=back_recv.at[part],
                device_id=far_place(2 * k),
                device_id_type=MESH,
            ).start()
            return carry

        lax.fori_loop(1, DEEP, give_back, 0)
        pieces.append(
            pltpu.make_async_remote_copy(
                src_ref=sent.at[pl.ds(1, DEEP - 1), :, lanes],
                dst_ref=back.at[pl.ds(1, DEEP - 1), :, lanes],
                send_sem=back_send.at[part],
                recv_sem=back_recv.at[part],
                device_id=far_place(2),
                device_id_type=MESH,
            )
        )
    columns = [0.0] * 4
    for part, piece in enumerate(pieces):
        piece.wait_recv()
        cut = slice(CUTS[part], CUTS[part + 1])
        d, r = d_ref[:, cut], r_ref[:, cut]
        image = p_ref[:, cut] + d
        for s in range(ROUNDS):
            image = image + jnp.where(depths[s] == 0, terms[s, :, cut], 0.0)
        for k in range(1, DEEP):
            image = image + back[k, :, cut].astype(F32)
        image_ref[:, cut] = image
        for q, (a, b) in enumerate(((r, r), (d, image), (r, image), (image, image))):
            columns[q] = columns[q] + jnp.sum(a * b, axis=1, keepdims=True)
    lane = lax.broadcasted_iota(jnp.int32, (8, 128), 1)
    packed = jnp.zeros((8, 128), F32)
    for q, column in enumerate(columns):
        for g in range(4):
            packed = jnp.where(lane == q * 4 + g, column[g * 8 : g * 8 + 8], packed)
    near[0] = packed
    first = exchange(near, near_send, near_recv, near_place)
    far[0] = tree(near)
    second = exchange(far, far_send, far_recv, far_place)
    total = tree(far)
    norm, curv, cross, square = (
        jnp.concatenate([total[:, q * 4 + g : q * 4 + g + 1] for g in range(4)], axis=0)
        for q in range(4)
    )
    alpha = norm / curv
    alpha_ref[...] = alpha
    twice, quad = 2.0 * alpha * cross, alpha * alpha * square
    following = norm - twice + quad
    good = following >= LOSS * (norm + jnp.abs(twice) + quad)
    good = jnp.logical_and(good, following < 3e38)
    beta_ref[...] = following / norm
    bad_ref[0, 0] = jnp.max(jnp.where(good, 0.0, 1.0))
    bad_ref[0, 1] = 0.0
    for piece in pieces:
        piece.wait_send()
    first.wait_send()
    second.wait_send()


def finish(depths, dir_t, res_t, prior_t, parts, blocks):
    column = jax.ShapeDtypeStruct((PROBES, 1), F32)
    dma = pltpu.SemaphoreType.DMA
    return pl.pallas_call(
        finish_kernel,
        out_shape=(
            jax.ShapeDtypeStruct((PROBES, ROWS), F32),
            column,
            column,
            jax.ShapeDtypeStruct((1, 2), F32),
        ),
        in_specs=[SMEM] + [VMEM] * 3 + [ANY] * 6,
        out_specs=(VMEM, VMEM, VMEM, SMEM),
        scratch_shapes=[pltpu.VMEM((DEEP, PART, DIM), BF16)] * 3
        + [pltpu.VMEM((ROUNDS, TALL, ROWS), BF16), pltpu.VMEM((ROUNDS, 1, ROWS), F32)]
        + [pltpu.VMEM((ROUNDS, PROBES, ROWS), F32)]
        + [pltpu.VMEM((DEEP, PROBES, ROWS), BF16)] * 2
        + [pltpu.VMEM((16, 8, 128), F32)] * 2
        + [dma((3,))] * 4 + [dma] * 4,
        compiler_params=params(1),
        name="finish",
    )(depths, dir_t, res_t, prior_t, *parts, *blocks)


def result_kernel(d_ref, r_ref, s_ref, image_ref, alpha_ref, beta_ref, ns_ref, nr_ref, nd_ref):
    d, alpha = d_ref[...], alpha_ref[...]
    ns_ref[...] = s_ref[...] + alpha * d
    new_residual = r_ref[...] - alpha * image_ref[...]
    nr_ref[...] = new_residual
    nd_ref[...] = new_residual + beta_ref[...] * d


def result(*operands):
    shape = jax.ShapeDtypeStruct((PROBES, ROWS), F32)
    return pl.pallas_call(
        result_kernel,
        out_shape=(shape,) * 3,
        in_specs=[VMEM] * 6,
        out_specs=(VMEM,) * 3,
        compiler_params=params(),
        name="result",
    )(*operands)


def local(embedding, direction, residual, solution, prior, plan, round_index):
    dir_t, res_t = direction.T, residual.T
    masks = lax.dynamic_slice(plan, (round_index[0],), (ROUNDS,))
    depths = jnp.bitwise_and(masks >> 4, DEEP - 1)
    rests = jnp.bitwise_or((masks >> 7) << 4, jnp.bitwise_and(masks, 15))
    block, *own = prepare(embedding, dir_t)
    parts, blocks = [], []
    for step in range(ROUNDS):
        part, arrived = move_by(rests[step], own[step], block)
        parts.append(part)
        blocks.append(arrived)
    image, alpha, beta, bad = finish(depths, dir_t, res_t, prior.T, parts, blocks)

    def again():
        new_res = res_t - alpha * image
        norm = lax.psum(jnp.sum(res_t * res_t, axis=1, keepdims=True), AXES)
        return lax.psum(jnp.sum(new_res * new_res, axis=1, keepdims=True), AXES) / norm

    beta = lax.cond(bad[0, 0] > 0, again, lambda: beta)
    results = result(dir_t, res_t, solution.T, image, alpha, beta)
    return tuple(out.T for out in results)


def solution(mesh):
    rows = P(AXES, None)
    return jax.shard_map(
        local,
        mesh=mesh,
        in_specs=(rows,) * 5 + (P(), P()),
        out_specs=(rows,) * 3,
        check_vma=False,
    )
```

```python
import functools
import math

import jax
import jax.numpy as jnp
from jax import lax
from jax.experimental import pallas as pl
from jax.experimental.pallas import tpu as pltpu
from jax.sharding import PartitionSpec as P


ROUNDS = 3
GAMMA = 2.0
ROWS = 1024
DIM = 512
PROBES = 32
DEEP = 8
AXES = ("blk", "grp")
MESH = pl.DeviceIdType.MESH
VMEM = pl.BlockSpec(memory_space=pltpu.VMEM)
SMEM = pl.BlockSpec(memory_space=pltpu.SMEM)
ANY = pl.BlockSpec(memory_space=pl.ANY)
F32 = jnp.float32
BF16 = jnp.bfloat16
TALL = DIM + PROBES
PART = 352
STARTS = (0, 336, 672)
HALF = PART // 2
PIECES = ((0, 96), (96, 80))
CUTS = (0, 256, 640, 1024)
SCALE = -GAMMA * math.log2(math.e)
LOSS = 1e-2


def params(collective_id=None):
    return pltpu.CompilerParams(
        collective_id=collective_id,
        has_side_effects=collective_id is not None,
        vmem_limit_bytes=40 * 2**20,
    )


def prepare_kernel(x_ref, d_ref, out_ref, p0_ref, p1_ref, p2_ref):
    out_ref[:DIM] = x_ref[...].T
    out_ref[DIM:] = d_ref[...].astype(BF16)
    for ref, start in zip((p0_ref, p1_ref, p2_ref), STARTS):
        ref[...] = x_ref[start : start + PART]


def prepare(embedding, dir_t):
    part = jax.ShapeDtypeStruct((PART, DIM), BF16)
    return pl.pallas_call(
        prepare_kernel,
        out_shape=(jax.ShapeDtypeStruct((TALL, ROWS), BF16), part, part, part),
        in_specs=[VMEM] * 2,
        out_specs=(VMEM,) * 4,
        compiler_params=params(),
        name="prepare",
    )(embedding, dir_t)


def move_kernel(
    rest, part_ref, block_ref, ring_ref, b_ref, own_sem, b_send, b_recv, ring_send, ring_recv
):
    blk, grp = lax.axis_index("blk"), lax.axis_index("grp")
    z = (blk >> 1) & (DEEP - 1)
    base = blk - 2 * z
    other = (blk ^ ((rest >> 4) << 4 | (rest >> 3) & 1), grp ^ (rest & 7))

    def along(way):
        return (base + 2 * ((z + way) & (DEEP - 1)), grp)

    barrier = pltpu.get_barrier_semaphore()

    def greet(index, carry):
        device = along(1 + index * (DEEP - 2))
        pl.semaphore_signal(barrier, inc=1, device_id=device, device_id_type=MESH)
        return carry

    lax.fori_loop(0, 2, greet, 0)
    if rest:
        pl.semaphore_signal(barrier, inc=1, device_id=other, device_id_type=MESH)
    own = pltpu.make_async_copy(part_ref, ring_ref.at[0], own_sem)
    own.start()
    pl.semaphore_wait(barrier, 3 if rest else 2)

    def hop(index, step, half, piece):
        way = 1 + index * (DEEP - 2)
        rows = pl.ds(half * HALF + PIECES[piece][0], PIECES[piece][1])
        return pltpu.make_async_remote_copy(
            src_ref=ring_ref.at[(way * (step - 1)) & (DEEP - 1), rows],
            dst_ref=ring_ref.at[(way * step) & (DEEP - 1), rows],
            send_sem=ring_send.at[index, step >> 2],
            recv_sem=ring_recv.at[index, 4 * (step - 1) + 2 * half + piece],
            device_id=along(way),
            device_id_type=MESH,
        )

    if rest:
        direct = pltpu.make_async_remote_copy(
            src_ref=block_ref,
            dst_ref=b_ref,
            send_sem=b_send,
            recv_sem=b_recv,
            device_id=other,
            device_id_type=MESH,
        )
    else:
        direct = pltpu.make_async_copy(block_ref, b_ref, b_send)
    direct.start()
    own.wait()

    def pass_on(count, carry):
        step, index = count >> 2, count & 1
        half = ((count >> 1) & 1) + index * (step >> 2)
        for piece in range(len(PIECES)):

            @pl.when(step > 1)
            def _():
                hop(index, step - 1, half, piece).wait_recv()

            hop(index, step, half, piece).start()
        return carry

    lax.fori_loop(4, 18, pass_on, 0)

    def drain(index, carry):
        for piece in range(len(PIECES)):
            hop(index, 3, 1 - index, piece).wait_recv()
            hop(index, 4, index, piece).wait_recv()
        for which, whole in enumerate((ring_ref.at[pl.ds(0, 3)], ring_ref.at[0, pl.ds(0, HALF)])):
            pltpu.make_async_remote_copy(
                src_ref=whole,
                dst_ref=whole,
                send_sem=ring_send.at[index, which],
                recv_sem=ring_recv.at[0, 0],
                device_id=along(1),
                device_id_type=MESH,
            ).wait_send()
        return carry

    lax.fori_loop(0, 2, drain, 0)
    direct.wait()


def move(rest, part, block):
    one = pltpu.SemaphoreType.DMA
    return pl.pallas_call(
        functools.partial(move_kernel, rest),
        out_shape=(
            jax.ShapeDtypeStruct((DEEP, PART, DIM), BF16),
            jax.ShapeDtypeStruct((TALL, ROWS), BF16),
        ),
        in_specs=[ANY] * 2,
        out_specs=(ANY, ANY),
        scratch_shapes=[one, one, one, one((2, 2)), one((2, 16))],
        compiler_params=params(2 + rest),
        name=f"move_{rest}",
    )(part, block)


def move_by(rest, part, block):
    return lax.switch(rest, [functools.partial(move, k) for k in range(32)], part, block)


def tree(ref):
    v = ref[...]
    while v.shape[0] > 1:
        half = v.shape[0] // 2
        v = v[:half] + v[half:]
    return v[0]


def exchange(slots, send_sem, recv_sem, place):
    count = slots.shape[0]

    def send(k, carry):
        pltpu.make_async_remote_copy(
            src_ref=slots.at[0],
            dst_ref=slots.at[k],
            send_sem=send_sem,
            recv_sem=recv_sem,
            device_id=place(k),
            device_id_type=MESH,
        ).start()
        return carry

    lax.fori_loop(1, count, send, 0)
    whole = pltpu.make_async_remote_copy(
        src_ref=slots.at[pl.ds(1, count - 1)],
        dst_ref=slots.at[pl.ds(1, count - 1)],
        send_sem=send_sem,
        recv_sem=recv_sem,
        device_id=place(1),
        device_id_type=MESH,
    )
    whole.wait_recv()
    return whole


def finish_kernel(
    depth_ref, d_ref, r_ref, p_ref, g0_ref, g1_ref, g2_ref, b0_ref, b1_ref, b2_ref,
    image_ref, alpha_ref, beta_ref, bad_ref,
    g0, g1, g2, blocks, right_sq, terms, sent, back, near, far,
    part_sem, block_sem, back_send, back_recv, near_send, near_recv, far_send, far_recv,
):
    blk, grp = lax.axis_index("blk"), lax.axis_index("grp")
    z = lax.rem(lax.div(blk, 2), DEEP)

    def near_place(k):
        return (blk ^ ((k >> 3) << 4), grp ^ (k & 7))

    def far_place(k):
        return (blk ^ k, grp)

    barrier = pltpu.get_barrier_semaphore()

    def greet(k, carry):
        pl.semaphore_signal(barrier, inc=1, device_id=near_place(k), device_id_type=MESH)
        pl.semaphore_signal(barrier, inc=1, device_id=far_place(k), device_id_type=MESH)
        return carry

    for k in range(1, 16):
        greet(k, 0)

    def load_block(s):
        return pltpu.make_async_copy((b0_ref, b1_ref, b2_ref)[s], blocks.at[s], block_sem.at[s])

    def load_part(part):
        refs = ((g0_ref, g0), (g1_ref, g1), (g2_ref, g2))
        return pltpu.make_async_copy(*refs[part], part_sem.at[part])

    load_block(0).start()
    load_part(0).start()
    for s in range(1, ROUNDS):
        load_block(s).start()
    depths = [depth_ref[s] for s in range(ROUNDS)]
    pieces = []
    for part, gathered in enumerate((g0, g1, g2)):
        load_part(part).wait()
        if part + 1 < ROUNDS:
            load_part(part + 1).start()

        def one_term(s, carry, part=part, gathered=gathered):
            if part == 0:
                pltpu.make_async_copy(b0_ref, blocks.at[s], block_sem.at[s]).wait()
                wide = blocks[s, :DIM].astype(F32)
                right_sq[s] = SCALE * jnp.sum(wide * wide, axis=0, keepdims=True)
            slot = (z - (z ^ depth_ref[s])) & (DEEP - 1)
            a = gathered[slot]
            wide = a.astype(F32)
            left_sq = SCALE * jnp.sum(wide * wide, axis=1, keepdims=True) + 1.0
            cross = jnp.dot(a, blocks[s, :DIM], preferred_element_type=F32)
            kern = jnp.exp2((left_sq + right_sq[s]) + (-2.0 * SCALE) * cross).astype(BF16)
            terms[s, :, STARTS[part] : STARTS[part] + PART] = lax.dot_general(
                blocks[s, DIM:], kern, (((1,), (1,)), ((), ())), preferred_element_type=F32
            )
            return carry

        lax.fori_loop(0, ROUNDS, one_term, 0)
        columns = slice(CUTS[part], CUTS[part + 1])
        lanes = pl.ds(CUTS[part], CUTS[part + 1] - CUTS[part])
        if part == 0:
            pl.semaphore_wait(barrier, 30)

        def give_back(k, carry, part=part, columns=columns, lanes=lanes):
            meant = sum(
                jnp.where(depths[s] == k, terms[s, :, columns], 0.0) for s in range(ROUNDS)
            )
            sent[k, :, columns] = meant.astype(BF16)
            pltpu.make_async_remote_copy(
                src_ref=sent.at[k, :, lanes],
                dst_ref=back.at[k, :, lanes],
                send_sem=back_send.at[part],
                recv_sem=back_recv.at[part],
                device_id=far_place(2 * k),
                device_id_type=MESH,
            ).start()
            return carry

        lax.fori_loop(1, DEEP, give_back, 0)
        pieces.append(
            pltpu.make_async_remote_copy(
                src_ref=sent.at[pl.ds(1, DEEP - 1), :, lanes],
                dst_ref=back.at[pl.ds(1, DEEP - 1), :, lanes],
                send_sem=back_send.at[part],
                recv_sem=back_recv.at[part],
                device_id=far_place(2),
                device_id_type=MESH,
            )
        )
    columns = [0.0] * 4
    for part, piece in enumerate(pieces):
        piece.wait_recv()
        cut = slice(CUTS[part], CUTS[part + 1])
        d, r = d_ref[:, cut], r_ref[:, cut]
        image = p_ref[:, cut] + d
        for s in range(ROUNDS):
            image = image + jnp.where(depths[s] == 0, terms[s, :, cut], 0.0)
        for k in range(1, DEEP):
            image = image + back[k, :, cut].astype(F32)
        image_ref[:, cut] = image
        for q, (a, b) in enumerate(((r, r), (d, image), (r, image), (image, image))):
            columns[q] = columns[q] + jnp.sum(a * b, axis=1, keepdims=True)
    lane = lax.broadcasted_iota(jnp.int32, (8, 128), 1)
    packed = jnp.zeros((8, 128), F32)
    for q, column in enumerate(columns):
        for g in range(4):
            packed = jnp.where(lane == q * 4 + g, column[g * 8 : g * 8 + 8], packed)
    near[0] = packed
    first = exchange(near, near_send, near_recv, near_place)
    far[0] = tree(near)
    second = exchange(far, far_send, far_recv, far_place)
    total = tree(far)
    norm, curv, cross, square = (
        jnp.concatenate([total[:, q * 4 + g : q * 4 + g + 1] for g in range(4)], axis=0)
        for q in range(4)
    )
    alpha = norm / curv
    alpha_ref[...] = alpha
    twice, quad = 2.0 * alpha * cross, alpha * alpha * square
    following = norm - twice + quad
    good = following >= LOSS * (norm + jnp.abs(twice) + quad)
    good = jnp.logical_and(good, following < 3e38)
    beta_ref[...] = following / norm
    bad_ref[0, 0] = jnp.max(jnp.where(good, 0.0, 1.0))
    bad_ref[0, 1] = 0.0
    for piece in pieces:
        piece.wait_send()
    first.wait_send()
    second.wait_send()


def finish(depths, dir_t, res_t, prior_t, parts, blocks):
    column = jax.ShapeDtypeStruct((PROBES, 1), F32)
    dma = pltpu.SemaphoreType.DMA
    return pl.pallas_call(
        finish_kernel,
        out_shape=(
            jax.ShapeDtypeStruct((PROBES, ROWS), F32),
            column,
            column,
            jax.ShapeDtypeStruct((1, 2), F32),
        ),
        in_specs=[SMEM] + [VMEM] * 3 + [ANY] * 6,
        out_specs=(VMEM, VMEM, VMEM, SMEM),
        scratch_shapes=[pltpu.VMEM((DEEP, PART, DIM), BF16)] * 3
        + [pltpu.VMEM((ROUNDS, TALL, ROWS), BF16), pltpu.VMEM((ROUNDS, 1, ROWS), F32)]
        + [pltpu.VMEM((ROUNDS, PROBES, ROWS), F32)]
        + [pltpu.VMEM((DEEP, PROBES, ROWS), BF16)] * 2
        + [pltpu.VMEM((16, 8, 128), F32)] * 2
        + [dma((3,))] * 4 + [dma] * 4,
        compiler_params=params(1),
        name="finish",
    )(depths, dir_t, res_t, prior_t, *parts, *blocks)


def result_kernel(d_ref, r_ref, s_ref, image_ref, alpha_ref, beta_ref, ns_ref, nr_ref, nd_ref):
    d, alpha = d_ref[...], alpha_ref[...]
    ns_ref[...] = s_ref[...] + alpha * d
    new_residual = r_ref[...] - alpha * image_ref[...]
    nr_ref[...] = new_residual
    nd_ref[...] = new_residual + beta_ref[...] * d


def result(*operands):
    shape = jax.ShapeDtypeStruct((PROBES, ROWS), F32)
    return pl.pallas_call(
        result_kernel,
        out_shape=(shape,) * 3,
        in_specs=[VMEM] * 6,
        out_specs=(VMEM,) * 3,
        compiler_params=params(),
        name="result",
    )(*operands)


def local(embedding, direction, residual, solution, prior, plan, round_index):
    dir_t, res_t = direction.T, residual.T
    masks = lax.dynamic_slice(plan, (round_index[0],), (ROUNDS,))
    depths = jnp.bitwise_and(masks >> 4, DEEP - 1)
    rests = jnp.bitwise_or((masks >> 7) << 4, jnp.bitwise_and(masks, 15))
    block, *own = prepare(embedding, dir_t)
    parts, blocks = [], []
    for step in range(ROUNDS):
        part, arrived = move_by(rests[step], own[step], block)
        parts.append(part)
        blocks.append(arrived)
    image, alpha, beta, bad = finish(depths, dir_t, res_t, prior.T, parts, blocks)

    def again():
        new_res = res_t - alpha * image
        norm = lax.psum(jnp.sum(res_t * res_t, axis=1, keepdims=True), AXES)
        return lax.psum(jnp.sum(new_res * new_res, axis=1, keepdims=True), AXES) / norm

    beta = lax.cond(bad[0, 0] > 0, again, lambda: beta)
    results = result(dir_t, res_t, solution.T, image, alpha, beta)
    return tuple(out.T for out in results)


def solution(mesh):
    rows = P(AXES, None)
    return jax.shard_map(
        local,
        mesh=mesh,
        in_specs=(rows,) * 5 + (P(), P()),
        out_specs=(rows,) * 3,
        check_vma=False,
    )
```

```python
import functools
import math

import jax
import jax.numpy as jnp
from jax import lax
from jax.experimental import pallas as pl
from jax.experimental.pallas import tpu as pltpu
from jax.sharding import PartitionSpec as P


ROUNDS = 3
GAMMA = 2.0
ROWS = 1024
DIM = 512
PROBES = 32
DEEP = 8
AXES = ("blk", "grp")
MESH = pl.DeviceIdType.MESH
VMEM = pl.BlockSpec(memory_space=pltpu.VMEM)
SMEM = pl.BlockSpec(memory_space=pltpu.SMEM)
ANY = pl.BlockSpec(memory_space=pl.ANY)
F32 = jnp.float32
BF16 = jnp.bfloat16
TALL = DIM + PROBES
PART = 352
STARTS = (0, 336, 672)
HALF = PART // 2
PIECES = ((0, 96), (96, 80))
CUTS = (0, 256, 640, 1024)
SCALE = -GAMMA * math.log2(math.e)
LOSS = 1e-2
TINY = 1e-25


def params(collective_id=None):
    return pltpu.CompilerParams(
        collective_id=collective_id,
        has_side_effects=collective_id is not None,
        vmem_limit_bytes=40 * 2**20,
    )


def prepare_kernel(x_ref, d_ref, out_ref, p0_ref, p1_ref, p2_ref):
    out_ref[:DIM] = x_ref[...].T
    out_ref[DIM:] = d_ref[...].astype(BF16)
    for ref, start in zip((p0_ref, p1_ref, p2_ref), STARTS):
        ref[...] = x_ref[start : start + PART]


def prepare(embedding, dir_t):
    part = jax.ShapeDtypeStruct((PART, DIM), BF16)
    return pl.pallas_call(
        prepare_kernel,
        out_shape=(jax.ShapeDtypeStruct((TALL, ROWS), BF16), part, part, part),
        in_specs=[VMEM] * 2,
        out_specs=(VMEM,) * 4,
        compiler_params=params(),
        name="prepare",
    )(embedding, dir_t)


def move_kernel(
    rest, part_ref, block_ref, ring_ref, b_ref, own_sem, b_send, b_recv, ring_send, ring_recv
):
    blk, grp = lax.axis_index("blk"), lax.axis_index("grp")
    z = (blk >> 1) & (DEEP - 1)
    base = blk - 2 * z
    other = (blk ^ ((rest >> 4) << 4 | (rest >> 3) & 1), grp ^ (rest & 7))

    def along(way):
        return (base + 2 * ((z + way) & (DEEP - 1)), grp)

    barrier = pltpu.get_barrier_semaphore()

    def greet(index, carry):
        device = along(1 + index * (DEEP - 2))
        pl.semaphore_signal(barrier, inc=1, device_id=device, device_id_type=MESH)
        return carry

    lax.fori_loop(0, 2, greet, 0)
    if rest:
        pl.semaphore_signal(barrier, inc=1, device_id=other, device_id_type=MESH)
    own = pltpu.make_async_copy(part_ref, ring_ref.at[0], own_sem)
    own.start()
    pl.semaphore_wait(barrier, 3 if rest else 2)

    def hop(index, step, half, piece):
        way = 1 + index * (DEEP - 2)
        rows = pl.ds(half * HALF + PIECES[piece][0], PIECES[piece][1])
        return pltpu.make_async_remote_copy(
            src_ref=ring_ref.at[(way * (step - 1)) & (DEEP - 1), rows],
            dst_ref=ring_ref.at[(way * step) & (DEEP - 1), rows],
            send_sem=ring_send.at[index, step >> 2],
            recv_sem=ring_recv.at[index, 4 * (step - 1) + 2 * half + piece],
            device_id=along(way),
            device_id_type=MESH,
        )

    if rest:
        direct = pltpu.make_async_remote_copy(
            src_ref=block_ref,
            dst_ref=b_ref,
            send_sem=b_send,
            recv_sem=b_recv,
            device_id=other,
            device_id_type=MESH,
        )
    else:
        direct = pltpu.make_async_copy(block_ref, b_ref, b_send)
    direct.start()
    own.wait()

    def pass_on(count, carry):
        step, index = count >> 2, count & 1
        half = ((count >> 1) & 1) + index * (step >> 2)
        for piece in range(len(PIECES)):

            @pl.when(step > 1)
            def _():
                hop(index, step - 1, half, piece).wait_recv()

            hop(index, step, half, piece).start()
        return carry

    lax.fori_loop(4, 18, pass_on, 0)

    def drain(index, carry):
        for piece in range(len(PIECES)):
            hop(index, 3, 1 - index, piece).wait_recv()
            hop(index, 4, index, piece).wait_recv()
        for which, whole in enumerate((ring_ref.at[pl.ds(0, 3)], ring_ref.at[0, pl.ds(0, HALF)])):
            pltpu.make_async_remote_copy(
                src_ref=whole,
                dst_ref=whole,
                send_sem=ring_send.at[index, which],
                recv_sem=ring_recv.at[0, 0],
                device_id=along(1),
                device_id_type=MESH,
            ).wait_send()
        return carry

    lax.fori_loop(0, 2, drain, 0)
    direct.wait()


def move(rest, part, block):
    one = pltpu.SemaphoreType.DMA
    return pl.pallas_call(
        functools.partial(move_kernel, rest),
        out_shape=(
            jax.ShapeDtypeStruct((DEEP, PART, DIM), BF16),
            jax.ShapeDtypeStruct((TALL, ROWS), BF16),
        ),
        in_specs=[ANY] * 2,
        out_specs=(ANY, ANY),
        scratch_shapes=[one, one, one, one((2, 2)), one((2, 16))],
        compiler_params=params(2 + rest),
        name=f"move_{rest}",
    )(part, block)


def move_by(rest, part, block):
    return lax.switch(rest, [functools.partial(move, k) for k in range(32)], part, block)


def tree(ref):
    v = ref[...]
    while v.shape[0] > 1:
        half = v.shape[0] // 2
        v = v[:half] + v[half:]
    return v[0]


def exchange(slots, send_sem, recv_sem, place):
    count = slots.shape[0]

    def send(k, carry):
        pltpu.make_async_remote_copy(
            src_ref=slots.at[0],
            dst_ref=slots.at[k],
            send_sem=send_sem,
            recv_sem=recv_sem,
            device_id=place(k),
            device_id_type=MESH,
        ).start()
        return carry

    lax.fori_loop(1, count, send, 0)
    whole = pltpu.make_async_remote_copy(
        src_ref=slots.at[pl.ds(1, count - 1)],
        dst_ref=slots.at[pl.ds(1, count - 1)],
        send_sem=send_sem,
        recv_sem=recv_sem,
        device_id=place(1),
        device_id_type=MESH,
    )
    whole.wait_recv()
    return whole


def finish_kernel(
    depth_ref, d_ref, r_ref, p_ref, g0_ref, g1_ref, g2_ref, b0_ref, b1_ref, b2_ref,
    image_ref, alpha_ref, beta_ref, bad_ref,
    g0, g1, g2, blocks, right_sq, terms, sent, back, near, far,
    part_sem, block_sem, back_send, back_recv, near_send, near_recv, far_send, far_recv,
):
    blk, grp = lax.axis_index("blk"), lax.axis_index("grp")
    z = lax.rem(lax.div(blk, 2), DEEP)

    def near_place(k):
        return (blk ^ ((k >> 3) << 4), grp ^ (k & 7))

    def far_place(k):
        return (blk ^ k, grp)

    barrier = pltpu.get_barrier_semaphore()

    def greet(k, carry):
        pl.semaphore_signal(barrier, inc=1, device_id=near_place(k), device_id_type=MESH)
        pl.semaphore_signal(barrier, inc=1, device_id=far_place(k), device_id_type=MESH)
        return carry

    for k in range(1, 16):
        greet(k, 0)

    def load_block(s):
        return pltpu.make_async_copy((b0_ref, b1_ref, b2_ref)[s], blocks.at[s], block_sem.at[s])

    def load_part(part):
        refs = ((g0_ref, g0), (g1_ref, g1), (g2_ref, g2))
        return pltpu.make_async_copy(*refs[part], part_sem.at[part])

    load_block(0).start()
    load_part(0).start()
    for s in range(1, ROUNDS):
        load_block(s).start()
    depths = [depth_ref[s] for s in range(ROUNDS)]
    pieces = []
    for part, gathered in enumerate((g0, g1, g2)):
        load_part(part).wait()
        if part + 1 < ROUNDS:
            load_part(part + 1).start()

        def one_term(s, carry, part=part, gathered=gathered):
            if part == 0:
                pltpu.make_async_copy(b0_ref, blocks.at[s], block_sem.at[s]).wait()
                wide = blocks[s, :DIM].astype(F32)
                right_sq[s] = SCALE * jnp.sum(wide * wide, axis=0, keepdims=True)
            slot = (z - (z ^ depth_ref[s])) & (DEEP - 1)
            a = gathered[slot]
            wide = a.astype(F32)
            left_sq = SCALE * jnp.sum(wide * wide, axis=1, keepdims=True) + 1.0
            cross = jnp.dot(a, blocks[s, :DIM], preferred_element_type=F32)
            kern = jnp.exp2((left_sq + right_sq[s]) + (-2.0 * SCALE) * cross).astype(BF16)
            terms[s, :, STARTS[part] : STARTS[part] + PART] = lax.dot_general(
                blocks[s, DIM:], kern, (((1,), (1,)), ((), ())), preferred_element_type=F32
            )
            return carry

        lax.fori_loop(0, ROUNDS, one_term, 0)
        columns = slice(CUTS[part], CUTS[part + 1])
        lanes = pl.ds(CUTS[part], CUTS[part + 1] - CUTS[part])
        if part == 0:
            pl.semaphore_wait(barrier, 30)

        def give_back(count, carry, part=part, columns=columns, lanes=lanes):
            k = lax.rem(count + 2, DEEP - 1) + 1
            meant = sum(
                jnp.where(depths[s] == k, terms[s, :, columns], 0.0) for s in range(ROUNDS)
            )
            sent[k, :, columns] = meant.astype(BF16)
            pltpu.make_async_remote_copy(
                src_ref=sent.at[k, :, lanes],
                dst_ref=back.at[k, :, lanes],
                send_sem=back_send.at[part],
                recv_sem=back_recv.at[part],
                device_id=far_place(2 * k),
                device_id_type=MESH,
            ).start()
            return carry

        lax.fori_loop(1, DEEP, give_back, 0)
        pieces.append(
            pltpu.make_async_remote_copy(
                src_ref=sent.at[pl.ds(1, DEEP - 1), :, lanes],
                dst_ref=back.at[pl.ds(1, DEEP - 1), :, lanes],
                send_sem=back_send.at[part],
                recv_sem=back_recv.at[part],
                device_id=far_place(2),
                device_id_type=MESH,
            )
        )
    columns = [0.0] * 4
    for part, piece in enumerate(pieces):
        piece.wait_recv()
        cut = slice(CUTS[part], CUTS[part + 1])
        d, r = d_ref[:, cut], r_ref[:, cut]
        image = p_ref[:, cut] + d
        for s in range(ROUNDS):
            image = image + jnp.where(depths[s] == 0, terms[s, :, cut], 0.0)
        for k in range(1, DEEP):
            image = image + back[k, :, cut].astype(F32)
        image_ref[:, cut] = image
        for q, (a, b) in enumerate(((r, r), (d, image), (r, image), (image, image))):
            columns[q] = columns[q] + jnp.sum(a * b, axis=1, keepdims=True)
    near[0] = jnp.broadcast_to(jnp.concatenate(columns, axis=0), (128, 128)).T[:1]
    first = exchange(near, near_send, near_recv, near_place)
    far[0] = tree(near)
    second = exchange(far, far_send, far_recv, far_place)
    total = tree(far)
    column = jnp.broadcast_to(total, (128, 128)).T[:, :1]
    norm, curv, cross, square = (column[q * PROBES : (q + 1) * PROBES] for q in range(4))
    alpha = norm / curv
    alpha_ref[...] = alpha
    twice, quad = 2.0 * alpha * cross, alpha * (alpha * square)
    following = norm - twice + quad
    good = following >= LOSS * (norm + jnp.abs(twice) + quad)
    good = jnp.logical_and(good, following < 3e38)
    good = jnp.logical_and(good, jnp.minimum(norm, square) > TINY)
    beta_ref[...] = following / norm
    bad_ref[0, 0] = jnp.max(jnp.where(good, 0.0, 1.0))
    bad_ref[0, 1] = 0.0
    for piece in pieces:
        piece.wait_send()
    first.wait_send()
    second.wait_send()


def finish(depths, dir_t, res_t, prior_t, parts, blocks):
    column = jax.ShapeDtypeStruct((PROBES, 1), F32)
    dma = pltpu.SemaphoreType.DMA
    return pl.pallas_call(
        finish_kernel,
        out_shape=(
            jax.ShapeDtypeStruct((PROBES, ROWS), F32),
            column,
            column,
            jax.ShapeDtypeStruct((1, 2), F32),
        ),
        in_specs=[SMEM] + [VMEM] * 3 + [ANY] * 6,
        out_specs=(VMEM, VMEM, VMEM, SMEM),
        scratch_shapes=[pltpu.VMEM((DEEP, PART, DIM), BF16)] * 3
        + [pltpu.VMEM((ROUNDS, TALL, ROWS), BF16), pltpu.VMEM((ROUNDS, 1, ROWS), F32)]
        + [pltpu.VMEM((ROUNDS, PROBES, ROWS), F32)]
        + [pltpu.VMEM((DEEP, PROBES, ROWS), BF16)] * 2
        + [pltpu.VMEM((16, 1, 128), F32)] * 2
        + [dma((3,))] * 4 + [dma] * 4,
        compiler_params=params(1),
        name="finish",
    )(depths, dir_t, res_t, prior_t, *parts, *blocks)


def result_kernel(d_ref, r_ref, s_ref, image_ref, alpha_ref, beta_ref, ns_ref, nr_ref, nd_ref):
    d, alpha = d_ref[...], alpha_ref[...]
    ns_ref[...] = s_ref[...] + alpha * d
    new_residual = r_ref[...] - alpha * image_ref[...]
    nr_ref[...] = new_residual
    nd_ref[...] = new_residual + beta_ref[...] * d


def result(*operands):
    shape = jax.ShapeDtypeStruct((PROBES, ROWS), F32)
    return pl.pallas_call(
        result_kernel,
        out_shape=(shape,) * 3,
        in_specs=[VMEM] * 6,
        out_specs=(VMEM,) * 3,
        compiler_params=params(),
        name="result",
    )(*operands)


def local(embedding, direction, residual, solution, prior, plan, round_index):
    dir_t, res_t = direction.T, residual.T
    masks = lax.dynamic_slice(plan, (round_index[0],), (ROUNDS,))
    depths = jnp.bitwise_and(masks >> 4, DEEP - 1)
    rests = jnp.bitwise_or((masks >> 7) << 4, jnp.bitwise_and(masks, 15))
    block, *own = prepare(embedding, dir_t)
    parts, blocks = [], []
    for step in range(ROUNDS):
        part, arrived = move_by(rests[step], own[step], block)
        parts.append(part)
        blocks.append(arrived)
    image, alpha, beta, bad = finish(depths, dir_t, res_t, prior.T, parts, blocks)

    def again():
        new_res = res_t - alpha * image
        norm = lax.psum(jnp.sum(res_t * res_t, axis=1, keepdims=True), AXES)
        return lax.psum(jnp.sum(new_res * new_res, axis=1, keepdims=True), AXES) / norm

    beta = lax.cond(bad[0, 0] > 0, again, lambda: beta)
    results = result(dir_t, res_t, solution.T, image, alpha, beta)
    return tuple(out.T for out in results)


def solution(mesh):
    rows = P(AXES, None)
    return jax.shard_map(
        local,
        mesh=mesh,
        in_specs=(rows,) * 5 + (P(), P()),
        out_specs=(rows,) * 3,
        check_vma=False,
    )
```

```python
import functools
import math

import jax
import jax.numpy as jnp
from jax import lax
from jax.experimental import pallas as pl
from jax.experimental.pallas import tpu as pltpu
from jax.sharding import PartitionSpec as P


ROUNDS = 3
GAMMA = 2.0
ROWS = 1024
DIM = 512
PROBES = 32
DEEP = 8
AXES = ("blk", "grp")
MESH = pl.DeviceIdType.MESH
VMEM = pl.BlockSpec(memory_space=pltpu.VMEM)
SMEM = pl.BlockSpec(memory_space=pltpu.SMEM)
ANY = pl.BlockSpec(memory_space=pl.ANY)
F32 = jnp.float32
BF16 = jnp.bfloat16
TALL = DIM + PROBES
PART = 352
STARTS = (0, 336, 672)
HALF = PART // 2
PIECES = ((0, 96), (96, 80))
CUTS = (0, 256, 512, 1024)
SCALE = -GAMMA * math.log2(math.e)
LOSS = 1e-2
TINY = 1e-25


def params(collective_id=None):
    return pltpu.CompilerParams(
        collective_id=collective_id,
        has_side_effects=collective_id is not None,
        vmem_limit_bytes=40 * 2**20,
    )


def prepare_kernel(x_ref, d_ref, out_ref, p0_ref, p1_ref, p2_ref, x, d, sems):
    load_x = pltpu.make_async_copy(x_ref, x, sems.at[0])
    load_d = pltpu.make_async_copy(d_ref, d, sems.at[1])
    load_x.start()
    load_d.start()
    load_x.wait()
    out_ref[:DIM] = x[...].T
    for ref, start in zip((p0_ref, p1_ref, p2_ref), STARTS):
        ref[...] = x[start : start + PART]
    load_d.wait()
    out_ref[DIM:] = d[...].astype(BF16)


def prepare(embedding, dir_t):
    part = jax.ShapeDtypeStruct((PART, DIM), BF16)
    return pl.pallas_call(
        prepare_kernel,
        out_shape=(jax.ShapeDtypeStruct((TALL, ROWS), BF16), part, part, part),
        in_specs=[ANY] * 2,
        out_specs=(VMEM,) * 4,
        scratch_shapes=[
            pltpu.VMEM((ROWS, DIM), BF16),
            pltpu.VMEM((PROBES, ROWS), F32),
            pltpu.SemaphoreType.DMA((2,)),
        ],
        compiler_params=pltpu.CompilerParams(vmem_limit_bytes=60 * 2**20),
        name="prepare",
    )(embedding, dir_t)


def move_kernel(
    rest, part_ref, block_ref, ring_ref, b_ref, own_sem, b_send, b_recv, ring_send, ring_recv
):
    blk, grp = lax.axis_index("blk"), lax.axis_index("grp")
    z = (blk >> 1) & (DEEP - 1)
    base = blk - 2 * z
    other = (blk ^ ((rest >> 4) << 4 | (rest >> 3) & 1), grp ^ (rest & 7))

    def along(way):
        return (base + 2 * ((z + way) & (DEEP - 1)), grp)

    barrier = pltpu.get_barrier_semaphore()

    def greet(index, carry):
        device = along(1 + index * (DEEP - 2))
        pl.semaphore_signal(barrier, inc=1, device_id=device, device_id_type=MESH)
        return carry

    lax.fori_loop(0, 2, greet, 0)
    if rest:
        pl.semaphore_signal(barrier, inc=1, device_id=other, device_id_type=MESH)
    own = pltpu.make_async_copy(part_ref, ring_ref.at[0], own_sem)
    own.start()
    pl.semaphore_wait(barrier, 3 if rest else 2)

    def hop(index, step, half, piece):
        way = 1 + index * (DEEP - 2)
        rows = pl.ds(half * HALF + PIECES[piece][0], PIECES[piece][1])
        return pltpu.make_async_remote_copy(
            src_ref=ring_ref.at[(way * (step - 1)) & (DEEP - 1), rows],
            dst_ref=ring_ref.at[(way * step) & (DEEP - 1), rows],
            send_sem=ring_send.at[index, step >> 2],
            recv_sem=ring_recv.at[index, 4 * (step - 1) + 2 * half + piece],
            device_id=along(way),
            device_id_type=MESH,
        )

    if rest:
        direct = pltpu.make_async_remote_copy(
            src_ref=block_ref,
            dst_ref=b_ref,
            send_sem=b_send,
            recv_sem=b_recv,
            device_id=other,
            device_id_type=MESH,
        )
    else:
        direct = pltpu.make_async_copy(block_ref, b_ref, b_send)
    direct.start()
    own.wait()

    def pass_on(count, carry):
        step, index = count >> 2, count & 1
        half = ((count >> 1) & 1) + index * (step >> 2)
        for piece in range(len(PIECES)):

            @pl.when(step > 1)
            def _():
                hop(index, step - 1, half, piece).wait_recv()

            hop(index, step, half, piece).start()
        return carry

    lax.fori_loop(4, 18, pass_on, 0)

    def drain(index, carry):
        for piece in range(len(PIECES)):
            hop(index, 3, 1 - index, piece).wait_recv()
            hop(index, 4, index, piece).wait_recv()
        for which, whole in enumerate((ring_ref.at[pl.ds(0, 3)], ring_ref.at[0, pl.ds(0, HALF)])):
            pltpu.make_async_remote_copy(
                src_ref=whole,
                dst_ref=whole,
                send_sem=ring_send.at[index, which],
                recv_sem=ring_recv.at[0, 0],
                device_id=along(1),
                device_id_type=MESH,
            ).wait_send()
        return carry

    lax.fori_loop(0, 2, drain, 0)
    direct.wait()


def move(rest, part, block):
    one = pltpu.SemaphoreType.DMA
    return pl.pallas_call(
        functools.partial(move_kernel, rest),
        out_shape=(
            jax.ShapeDtypeStruct((DEEP, PART, DIM), BF16),
            jax.ShapeDtypeStruct((TALL, ROWS), BF16),
        ),
        in_specs=[ANY] * 2,
        out_specs=(ANY, ANY),
        scratch_shapes=[one, one, one, one((2, 2)), one((2, 16))],
        compiler_params=params(2 + rest),
        name=f"move_{rest}",
    )(part, block)


def move_by(rest, part, block):
    return lax.switch(rest, [functools.partial(move, k) for k in range(32)], part, block)


def tree(ref):
    v = ref[...]
    while v.shape[0] > 1:
        half = v.shape[0] // 2
        v = v[:half] + v[half:]
    return v[0]


def exchange(slots, send_sem, recv_sem, place):
    count = slots.shape[0]

    def send(k, carry):
        pltpu.make_async_remote_copy(
            src_ref=slots.at[0],
            dst_ref=slots.at[k],
            send_sem=send_sem,
            recv_sem=recv_sem,
            device_id=place(k),
            device_id_type=MESH,
        ).start()
        return carry

    lax.fori_loop(1, count, send, 0)
    whole = pltpu.make_async_remote_copy(
        src_ref=slots.at[pl.ds(1, count - 1)],
        dst_ref=slots.at[pl.ds(1, count - 1)],
        send_sem=send_sem,
        recv_sem=recv_sem,
        device_id=place(1),
        device_id_type=MESH,
    )
    whole.wait_recv()
    return whole


def finish_kernel(
    depth_ref, d_ref, r_ref, p_ref, g0_ref, g1_ref, g2_ref, b0_ref, b1_ref, b2_ref,
    image_ref, alpha_ref, beta_ref, bad_ref,
    g0, g1, g2, blocks, right_sq, terms, sent, back, near, far,
    part_sem, block_sem, back_send, back_recv, near_send, near_recv, far_send, far_recv,
):
    blk, grp = lax.axis_index("blk"), lax.axis_index("grp")
    z = lax.rem(lax.div(blk, 2), DEEP)

    def near_place(k):
        return (blk ^ ((k >> 3) << 4), grp ^ (k & 7))

    def far_place(k):
        return (blk ^ k, grp)

    barrier = pltpu.get_barrier_semaphore()

    def greet(k, carry):
        pl.semaphore_signal(barrier, inc=1, device_id=near_place(k), device_id_type=MESH)
        pl.semaphore_signal(barrier, inc=1, device_id=far_place(k), device_id_type=MESH)
        return carry

    for k in range(1, 16):
        greet(k, 0)

    def load_block(s):
        return pltpu.make_async_copy((b0_ref, b1_ref, b2_ref)[s], blocks.at[s], block_sem.at[s])

    def load_part(part):
        refs = ((g0_ref, g0), (g1_ref, g1), (g2_ref, g2))
        return pltpu.make_async_copy(*refs[part], part_sem.at[part])

    load_block(0).start()
    load_part(0).start()
    for s in range(1, ROUNDS):
        load_block(s).start()
    depths = [depth_ref[s] for s in range(ROUNDS)]
    pieces = []
    for part, gathered in enumerate((g0, g1, g2)):
        load_part(part).wait()
        if part + 1 < ROUNDS:
            load_part(part + 1).start()

        def one_term(s, carry, part=part, gathered=gathered):
            if part == 0:
                pltpu.make_async_copy(b0_ref, blocks.at[s], block_sem.at[s]).wait()
                wide = blocks[s, :DIM].astype(F32)
                right_sq[s] = SCALE * jnp.sum(wide * wide, axis=0, keepdims=True)
            slot = (z - (z ^ depth_ref[s])) & (DEEP - 1)
            a = gathered[slot]
            wide = a.astype(F32)
            left_sq = SCALE * jnp.sum(wide * wide, axis=1, keepdims=True) + 1.0
            cross = jnp.dot(a, blocks[s, :DIM], preferred_element_type=F32)
            kern = jnp.exp2((left_sq + right_sq[s]) + (-2.0 * SCALE) * cross).astype(BF16)
            terms[s, :, STARTS[part] : STARTS[part] + PART] = lax.dot_general(
                blocks[s, DIM:], kern, (((1,), (1,)), ((), ())), preferred_element_type=F32
            )
            return carry

        lax.fori_loop(0, ROUNDS, one_term, 0)
        columns = slice(CUTS[part], CUTS[part + 1])
        lanes = pl.ds(CUTS[part], CUTS[part + 1] - CUTS[part])
        if part == 0:
            pl.semaphore_wait(barrier, 30)

        def give_back(count, carry, part=part, columns=columns, lanes=lanes):
            k = lax.rem(count + 2, DEEP - 1) + 1
            meant = sum(
                jnp.where(depths[s] == k, terms[s, :, columns], 0.0) for s in range(ROUNDS)
            )
            sent[k, :, columns] = meant.astype(BF16)
            pltpu.make_async_remote_copy(
                src_ref=sent.at[k, :, lanes],
                dst_ref=back.at[k, :, lanes],
                send_sem=back_send.at[part],
                recv_sem=back_recv.at[part],
                device_id=far_place(2 * k),
                device_id_type=MESH,
            ).start()
            return carry

        lax.fori_loop(1, DEEP, give_back, 0)
        pieces.append(
            pltpu.make_async_remote_copy(
                src_ref=sent.at[pl.ds(1, DEEP - 1), :, lanes],
                dst_ref=back.at[pl.ds(1, DEEP - 1), :, lanes],
                send_sem=back_send.at[part],
                recv_sem=back_recv.at[part],
                device_id=far_place(2),
                device_id_type=MESH,
            )
        )
    columns = [0.0] * 4
    for part, piece in enumerate(pieces):
        piece.wait_recv()
        cut = slice(CUTS[part], CUTS[part + 1])
        d, r = d_ref[:, cut], r_ref[:, cut]
        image = p_ref[:, cut] + d
        for s in range(ROUNDS):
            image = image + jnp.where(depths[s] == 0, terms[s, :, cut], 0.0)
        for k in range(1, DEEP):
            image = image + back[k, :, cut].astype(F32)
        image_ref[:, cut] = image
        for q, (a, b) in enumerate(((r, r), (d, image), (r, image), (image, image))):
            columns[q] = columns[q] + jnp.sum(a * b, axis=1, keepdims=True)
    near[0] = jnp.broadcast_to(jnp.concatenate(columns, axis=0), (128, 128)).T[:1]
    first = exchange(near, near_send, near_recv, near_place)
    far[0] = tree(near)
    second = exchange(far, far_send, far_recv, far_place)
    total = tree(far)
    column = jnp.broadcast_to(total, (128, 128)).T[:, :1]
    norm, curv, cross, square = (column[q * PROBES : (q + 1) * PROBES] for q in range(4))
    alpha = norm / curv
    alpha_ref[...] = alpha
    twice, quad = 2.0 * alpha * cross, alpha * (alpha * square)
    following = norm - twice + quad
    good = following >= LOSS * (norm + jnp.abs(twice) + quad)
    good = jnp.logical_and(good, following < 3e38)
    good = jnp.logical_and(good, jnp.minimum(norm, square) > TINY)
    beta_ref[...] = following / norm
    bad_ref[0, 0] = jnp.max(jnp.where(good, 0.0, 1.0))
    bad_ref[0, 1] = 0.0
    for piece in pieces:
        piece.wait_send()
    first.wait_send()
    second.wait_send()


def finish(depths, dir_t, res_t, prior_t, parts, blocks):
    column = jax.ShapeDtypeStruct((PROBES, 1), F32)
    dma = pltpu.SemaphoreType.DMA
    return pl.pallas_call(
        finish_kernel,
        out_shape=(
            jax.ShapeDtypeStruct((PROBES, ROWS), F32),
            column,
            column,
            jax.ShapeDtypeStruct((1, 2), F32),
        ),
        in_specs=[SMEM] + [VMEM] * 3 + [ANY] * 6,
        out_specs=(VMEM, VMEM, VMEM, SMEM),
        scratch_shapes=[pltpu.VMEM((DEEP, PART, DIM), BF16)] * 3
        + [pltpu.VMEM((ROUNDS, TALL, ROWS), BF16), pltpu.VMEM((ROUNDS, 1, ROWS), F32)]
        + [pltpu.VMEM((ROUNDS, PROBES, ROWS), F32)]
        + [pltpu.VMEM((DEEP, PROBES, ROWS), BF16)] * 2
        + [pltpu.VMEM((16, 1, 128), F32)] * 2
        + [dma((3,))] * 4 + [dma] * 4,
        compiler_params=params(1),
        name="finish",
    )(depths, dir_t, res_t, prior_t, *parts, *blocks)


def result_kernel(d_ref, r_ref, s_ref, image_ref, alpha_ref, beta_ref, ns_ref, nr_ref, nd_ref):
    d, alpha = d_ref[...], alpha_ref[...]
    ns_ref[...] = s_ref[...] + alpha * d
    new_residual = r_ref[...] - alpha * image_ref[...]
    nr_ref[...] = new_residual
    nd_ref[...] = new_residual + beta_ref[...] * d


def result(*operands):
    shape = jax.ShapeDtypeStruct((PROBES, ROWS), F32)
    return pl.pallas_call(
        result_kernel,
        out_shape=(shape,) * 3,
        in_specs=[VMEM] * 6,
        out_specs=(VMEM,) * 3,
        compiler_params=params(),
        name="result",
    )(*operands)


def local(embedding, direction, residual, solution, prior, plan, round_index):
    dir_t, res_t = direction.T, residual.T
    masks = lax.dynamic_slice(plan, (round_index[0],), (ROUNDS,))
    depths = jnp.bitwise_and(masks >> 4, DEEP - 1)
    rests = jnp.bitwise_or((masks >> 7) << 4, jnp.bitwise_and(masks, 15))
    block, *own = prepare(embedding, dir_t)
    parts, blocks = [], []
    for step in range(ROUNDS):
        part, arrived = move_by(rests[step], own[step], block)
        parts.append(part)
        blocks.append(arrived)
    image, alpha, beta, bad = finish(depths, dir_t, res_t, prior.T, parts, blocks)

    def again():
        new_res = res_t - alpha * image
        norm = lax.psum(jnp.sum(res_t * res_t, axis=1, keepdims=True), AXES)
        return lax.psum(jnp.sum(new_res * new_res, axis=1, keepdims=True), AXES) / norm

    beta = lax.cond(bad[0, 0] > 0, again, lambda: beta)
    results = result(dir_t, res_t, solution.T, image, alpha, beta)
    return tuple(out.T for out in results)


def solution(mesh):
    rows = P(AXES, None)
    return jax.shard_map(
        local,
        mesh=mesh,
        in_specs=(rows,) * 5 + (P(), P()),
        out_specs=(rows,) * 3,
        check_vma=False,
    )
```
